512 devices in a mesh: lon: 64 (over z, y_hi, core), lat: 8 (over x, y_lo).
Axes of the slice: x: 4, y: 8 (y_hi: 4, y_lo: 2; y = y_hi * 2 + y_lo), z: 8, core: 2. Of those that a mesh axis runs over, the one named last changes fastest.
Arguments:
- patches: bfloat16 [64, 512, 276], P('lat', 'lon')
- query_weight: bfloat16 [1024, 512], P(None, 'lon')
- key_weight: bfloat16 [1024, 512], P(None, 'lon')
- value_weight: bfloat16 [1024, 512], P(None, 'lon'), may hold values from -0.1875 to 0.1875
- out_weight: bfloat16 [512, 1024], P(None, 'lon'), may hold values from -0.25 to 0.25
- embed_weight: bfloat16 [276, 1024], P(None, 'lon'), may hold values from -0.0390625 to 0.0390625
- cotangent: bfloat16 [64, 512, 1024], P('lat', 'lon'), may hold values from -6 to 6
Outputs:
- block_out: bfloat16 [64, 512, 1024], P('lat', 'lon')
- patch_grad: bfloat16 [64, 512, 276], P('lat', 'lon')
The draws below stay inside these ranges and needn't reach their ends.
All inputs are finite; a program needn't handle non-finite values.
Results may differ from the reference program's by a relative error of at most 0.025.
The reference program's roundings to bfloat16 on the way count: a program that leaves them out, or rounds other values in their place, can miss the bound.
Values may be sent and summed in bfloat16 or wider, within the bound.
A program may use at most 64 MiB of HBM per device.

```python
import math
import jax
import jax.numpy as jnp
from jax import lax

D = 1024
HEADS = 8
RAD = 6
PIN = 276
ROWS_DEV = 8
HH = 512
NR = 64
NC = 512
LATS = 58


def shared_base(key):
    return jnp.clip(jax.random.normal(key, (D, HH), jnp.float32), -4.0, 4.0)


def draw_query_weight(key, part):
    base = shared_base(key)
    return (base * D ** (-0.5)).astype(jnp.bfloat16)


def draw_key_weight(key, part):
    key = jax.random.fold_in(key, 2)
    own = jnp.clip(jax.random.normal(key, (D, HH), jnp.float32), -4.0, 4.0)
    mixed = own
    return (mixed * D ** (-0.5)).astype(jnp.bfloat16)


def draw_patches(key, part):
    key = jax.random.fold_in(key, 5)
    noise = jax.random.normal(key, (NR, NC, PIN), jnp.float32)
    field = noise
    return jnp.clip(field, -6.0, 6.0).astype(jnp.bfloat16)


def block_scale(rng, shape, shards, smallest, high):
    def one(position, parts):
        heights = jax.random.uniform(jax.random.fold_in(jax.random.fold_in(rng, 6), position), (parts,), jnp.float32, smallest / len(shards), high / len(shards))
        return jnp.repeat(jnp.exp(heights), shape[position] // parts).reshape((-1,) + (1,) * (len(shape) - position - 1))

    loudness = one(*shards[0])
    for cut in shards[1:]:
        loudness = loudness * one(*cut)
    return loudness


def scatter_about(rng, extent, deviation, bound, split=(), kind=jnp.bfloat16):
    gain = block_scale(rng, extent, split, -0.22, 0.18) if split else 1.0
    entries = jax.random.normal(rng, extent, jnp.float32) * deviation * gain
    return jnp.minimum(jnp.maximum(entries, -bound), bound).astype(kind)


def setup_inputs(seed: int = 0) -> dict:
    splits = jax.random.split(jax.random.key(seed), 8)
    patches = draw_patches(jax.random.fold_in(splits[7], 71), 0)
    query_weight = draw_query_weight(jax.random.fold_in(splits[7], 71), 0)
    key_weight = draw_key_weight(jax.random.fold_in(splits[7], 71), 0)
    value_weight = scatter_about(splits[3], (D, HH), D ** -0.5, 0.1875, ((1, 64),))
    out_weight = scatter_about(splits[4], (HH, D), HH ** -0.5, 0.25, ((1, 64),))
    embed_weight = scatter_about(splits[5], (PIN, D), (100 * PIN) ** -0.5, 0.0390625, ((1, 64),))
    cotangent = scatter_about(splits[6], (NR, NC, D), 1.0, 6.0, ((0, 8), (1, 64)))
    return dict(patches=patches, query_weight=query_weight, key_weight=key_weight, value_weight=value_weight, out_weight=out_weight, embed_weight=embed_weight, cotangent=cotangent)


def layer_norm(embedded):
    centre = lax.optimization_barrier(jnp.mean(embedded, axis=-1, keepdims=True))
    centred = embedded - centre
    inv_std = lax.rsqrt(lax.optimization_barrier(jnp.mean(centred * centred, axis=-1, keepdims=True)) + 1e-05)
    return (centred * inv_std, inv_std)

def head_dot(left, right):
    return jnp.einsum('rche,rche->rch', left.astype(jnp.float32), right.astype(jnp.float32), precision=lax.Precision.HIGHEST)

def head_scale(weight, grid):
    return jnp.einsum('rch,rche->rche', weight.astype(jnp.float32), grid.astype(jnp.float32), precision=lax.Precision.HIGHEST)

def window_pass(queries, grad_attn, key_ext, value_ext, key_ok):
    row_count, col_count, channels = queries.shape
    head_size = channels // HEADS
    reach = 2 * RAD + 1
    score_scale = 1.0 / math.sqrt(head_size)
    q_heads = queries.reshape(row_count, col_count, HEADS, head_size)
    g_heads = grad_attn.reshape(row_count, col_count, HEADS, head_size)

    def take_piece(slab, offset):
        return slab[:, offset:offset + col_count].reshape(row_count, col_count, HEADS, head_size)

    def first(carried, shift_row):
        key_slab = lax.dynamic_slice_in_dim(key_ext, shift_row, row_count, 0)
        value_slab = lax.dynamic_slice_in_dim(value_ext, shift_row, row_count, 0)
        raw = [head_dot(q_heads, take_piece(key_slab, offset)) for offset in range(reach)]
        slope = [head_dot(g_heads, take_piece(value_slab, offset)) for offset in range(reach)]
        return (carried, (jnp.stack(raw, -1), jnp.stack(slope, -1)))
    shifts = jnp.arange(reach, dtype=jnp.int32)
    unused, (scores, dprob) = lax.scan(first, jnp.int32(0), shifts)
    row_mask = jnp.stack([key_ok[shift:shift + row_count] for shift in range(reach)], 0)
    allowed = row_mask[:, :, None, None, None] > 0.5
    scores = jnp.where(allowed, scores * score_scale, -jnp.inf)
    row_top = lax.optimization_barrier(jnp.max(scores, axis=(0, 4), keepdims=True))
    exp_terms = jnp.exp(scores - row_top)
    row_total = lax.optimization_barrier(jnp.sum(exp_terms, axis=(0, 4), keepdims=True))
    prob = exp_terms / row_total
    row_delta = lax.optimization_barrier(jnp.sum(prob * dprob, axis=(0, 4)))
    dscore = lax.optimization_barrier((prob * (dprob - row_delta[None, :, :, :, None])).astype(jnp.bfloat16))
    prob_b = lax.optimization_barrier(prob.astype(jnp.bfloat16))
    head_zero = jnp.zeros((row_count, col_count, HEADS, head_size), jnp.float32)
    ext_zero = jnp.zeros(key_ext.shape, jnp.float32)

    def second(carried, shift_row):
        attended, grad_q, grad_k, grad_v = carried
        key_slab = lax.dynamic_slice_in_dim(key_ext, shift_row, row_count, 0)
        value_slab = lax.dynamic_slice_in_dim(value_ext, shift_row, row_count, 0)
        p_row = lax.dynamic_index_in_dim(prob_b, shift_row, 0, keepdims=False)
        s_row = lax.dynamic_index_in_dim(dscore, shift_row, 0, keepdims=False)
        slab_k = jnp.zeros((row_count, col_count + 2 * RAD, channels), jnp.float32)
        slab_v = jnp.zeros((row_count, col_count + 2 * RAD, channels), jnp.float32)
        for offset in range(reach):
            attended = attended + head_scale(p_row[..., offset], take_piece(value_slab, offset))
            grad_q = grad_q + head_scale(s_row[..., offset], take_piece(key_slab, offset))
            spread = ((0, 0), (offset, reach - 1 - offset), (0, 0))
            slab_k = slab_k + jnp.pad(head_scale(s_row[..., offset], q_heads).reshape(row_count, col_count, channels), spread)
            slab_v = slab_v + jnp.pad(head_scale(p_row[..., offset], g_heads).reshape(row_count, col_count, channels), spread)
        grad_k = lax.dynamic_update_slice_in_dim(grad_k, lax.dynamic_slice_in_dim(grad_k, shift_row, row_count, 0) + slab_k, shift_row, 0)
        grad_v = lax.dynamic_update_slice_in_dim(grad_v, lax.dynamic_slice_in_dim(grad_v, shift_row, row_count, 0) + slab_v, shift_row, 0)
        return ((attended, grad_q, grad_k, grad_v), None)
    (attended, grad_q, grad_k, grad_v), unused = lax.scan(second, (head_zero, head_zero, ext_zero, ext_zero), shifts)
    attended = attended.reshape(row_count, col_count, channels).astype(jnp.bfloat16)
    grad_q = (grad_q * score_scale).reshape(row_count, col_count, channels).astype(jnp.bfloat16)
    return (attended, grad_q, grad_k * score_scale, grad_v)

def reference(patches, query_weight, key_weight, value_weight, out_weight, embed_weight, cotangent):
    row_total, col_total, patch_width = patches.shape
    width = embed_weight.shape[1]
    channels = query_weight.shape[1]
    row_ids = jnp.arange(row_total, dtype=jnp.int32)
    row_valid = (row_ids < LATS).astype(jnp.float32)
    valid_cells = jnp.repeat(row_valid, col_total)[:, None]
    embedded = jnp.dot(patches.reshape(row_total * col_total, patch_width), embed_weight, preferred_element_type=jnp.float32)
    normal, inv_std = layer_norm(embedded)
    normed = normal.astype(jnp.bfloat16)

    def project(weight):
        return jnp.dot(normed, weight, preferred_element_type=jnp.float32).astype(jnp.bfloat16).reshape(row_total, col_total, channels)
    queries = project(query_weight)
    keys_grid = project(key_weight)
    values_grid = project(value_weight)
    masked = cotangent.reshape(row_total * col_total, width).astype(jnp.float32) * valid_cells
    grad_attn = jnp.dot(masked.astype(jnp.bfloat16), out_weight.T, preferred_element_type=jnp.float32)
    grad_attn = grad_attn.astype(jnp.bfloat16).reshape(row_total, col_total, channels)

    def widen(grid):
        looped = jnp.concatenate((grid[:, col_total - RAD:], grid, grid[:, :RAD]), axis=1)
        return jnp.pad(looped, ((RAD, RAD), (0, 0), (0, 0)))
    key_pad = widen(keys_grid)
    value_pad = widen(values_grid)
    ext_ids = jnp.arange(row_total + 2 * RAD, dtype=jnp.int32) - RAD
    ext_ok = ((ext_ids >= 0) & (ext_ids < LATS)).astype(jnp.float32)
    block = math.gcd(ROWS_DEV, 8)
    starts = (jnp.arange(row_total // block, dtype=jnp.int32) * block).astype(jnp.int32)

    def one_block(carried, start):
        grad_k, grad_v = carried
        q_block = lax.dynamic_slice_in_dim(queries, start, block, 0)
        g_block = lax.dynamic_slice_in_dim(grad_attn, start, block, 0)
        k_block = lax.dynamic_slice_in_dim(key_pad, start, block + 2 * RAD, 0)
        v_block = lax.dynamic_slice_in_dim(value_pad, start, block + 2 * RAD, 0)
        ok_block = lax.dynamic_slice_in_dim(ext_ok, start, block + 2 * RAD, 0)
        att_block, dq_block, dk_block, dv_block = window_pass(q_block, g_block, k_block, v_block, ok_block)
        grad_k = lax.dynamic_update_slice_in_dim(grad_k, lax.dynamic_slice_in_dim(grad_k, start, block + 2 * RAD, 0) + dk_block, start, 0)
        grad_v = lax.dynamic_update_slice_in_dim(grad_v, lax.dynamic_slice_in_dim(grad_v, start, block + 2 * RAD, 0) + dv_block, start, 0)
        return ((grad_k, grad_v), (att_block, dq_block))
    ext_zero = jnp.zeros((row_total + 2 * RAD, col_total + 2 * RAD, channels), jnp.float32)
    (key_sum, value_sum), (attended, grad_query) = lax.scan(one_block, (ext_zero, ext_zero), starts)

    def fold(padded):
        inner_part = padded[RAD:RAD + row_total]
        folded = inner_part[:, RAD:RAD + col_total]
        folded = folded.at[:, :RAD].add(inner_part[:, RAD + col_total:])
        folded = folded.at[:, col_total - RAD:].add(inner_part[:, :RAD])
        return folded.astype(jnp.bfloat16).reshape(row_total * col_total, channels)
    grad_key = fold(key_sum)
    grad_value = fold(value_sum)
    attended = attended.reshape(row_total * col_total, channels)
    grad_query = grad_query.reshape(row_total * col_total, channels)
    mixed = embedded + jnp.dot(attended, out_weight, preferred_element_type=jnp.float32)
    block_out = (mixed * valid_cells).astype(jnp.bfloat16).reshape(row_total, col_total, width)
    grad_normed = jnp.dot(grad_query, query_weight.T, preferred_element_type=jnp.float32)
    grad_normed = grad_normed + jnp.dot(grad_key, key_weight.T, preferred_element_type=jnp.float32)
    grad_normed = grad_normed + jnp.dot(grad_value, value_weight.T, preferred_element_type=jnp.float32)
    centre_grad = lax.optimization_barrier(jnp.mean(grad_normed, axis=-1, keepdims=True))
    along = lax.optimization_barrier(jnp.mean(grad_normed * normal, axis=-1, keepdims=True))
    grad_embed = (masked + inv_std * (grad_normed - centre_grad - normal * along)).astype(jnp.bfloat16)
    patch_grad = jnp.dot(grad_embed, embed_weight.T, preferred_element_type=jnp.float32)
    patch_grad = patch_grad.astype(jnp.bfloat16).reshape(row_total, col_total, patch_width)
    return (block_out, patch_grad)
```

```python
import functools
import math

import jax
import jax.numpy as jnp
from jax import lax
from jax.experimental import pallas as pl
from jax.experimental.pallas import tpu as pltpu
from jax.sharding import PartitionSpec as P

HEADS = 8
RAD = 6
PAD = 6
EPS = 1e-05
MESH = pl.DeviceIdType.MESH
F32 = jnp.float32
BF16 = jnp.bfloat16

SIDE = 8
OWN = SIDE * SIDE
RIM = RAD * SIDE
BAND = OWN + 2 * RIM
EXT = 3 * BAND
HERE = BAND + RIM

NT = (((1,), (1,)), ((), ()))
NN = (((1,), (0,)), ((), ()))


def dot_nt(left, right):
    return lax.dot_general(left, right, NT, preferred_element_type=F32)


def dot_nn(left, right):
    return lax.dot_general(left, right, NN, preferred_element_type=F32)


def kernel(
    sizes, p_ref, q_ref, k_ref, v_ref, o_ref, e_ref, c_ref, out_ref, grad_ref,
    ge, go, gk, gq, gv, wk, wq, wv, px, cx, sx, nx, qx, kx, vx, gx, emb, nor, inv, att, dq, dk, dv, bias,
    y_send, y_recv, z_send, z_recv, s_send, s_recv, h_send, h_recv,
):
    lons, lats_dev = sizes
    lon, lat = lax.axis_index("lon"), lax.axis_index("lat")
    core, yh, z = lax.rem(lon, 2), lax.rem(lon // 2, 4), lon // 8
    zs = lons // 8
    first_row = lat * SIDE
    lats = SIDE * lats_dev - PAD
    patch_width = p_ref.shape[1]
    width = c_ref.shape[1]
    half = width // 2

    parts = (ge, go, gk, gq, gv)

    ge[z, yh, core] = jnp.zeros(ge.shape[3:], BF16)
    ge[z, yh, core, :, 0:patch_width] = e_ref[...]
    go[z, yh, core] = o_ref[...]
    for store, source in ((gk, k_ref), (gq, q_ref), (gv, v_ref)):
        wide = source[...].astype(F32)
        store[z, yh, core] = jnp.concatenate([wide[:, :half], wide[:, half:]], axis=0).astype(BF16)
    px[HERE : HERE + OWN] = jnp.zeros((OWN, px.shape[1]), BF16)
    px[HERE : HERE + OWN, 0:patch_width] = p_ref[...]
    cx[HERE : HERE + OWN] = c_ref[...]

    around = [(a, b) for a in (-1, 0, 1) for b in (-1, 0, 1) if (a, b) != (0, 0)]

    def near(a, b):
        return (lax.rem(lon + lons + a, lons), lax.rem(lat + lats_dev + b, lats_dev))

    def at_y(d):
        return ((z * 4 + lax.rem(yh + d, 4)) * 2 + core, lat)

    def at_z(d):
        return ((lax.rem(z + d + zs, zs) * 4 + yh) * 2 + core, lat)

    sibling = (lon + 1 - 2 * core, lat)
    greeted = [near(a, b) for a, b in around] + [at_y(1), at_y(2), at_y(3), at_z(1), at_z(-1), sibling]
    barrier = pltpu.get_barrier_semaphore()
    for partner in greeted:
        pl.semaphore_signal(barrier, inc=1, device_id=partner, device_id_type=MESH)
    pl.semaphore_wait(barrier, len(greeted))

    def send(source, target, send_sem, recv_sem, partner):
        copy = pltpu.make_async_remote_copy(
            src_ref=source, dst_ref=target, send_sem=send_sem, recv_sem=recv_sem,
            device_id=partner, device_id_type=MESH,
        )
        copy.start()
        return copy

    sent = []

    first = []
    for w, part in enumerate(parts):
        block = part.at[z, yh, core]
        first.append([
            send(block, block, y_send.at[w, d - 1], y_recv.at[w, d - 1], at_y(d)) for d in (1, 2, 3)
        ])
        sent.extend(first[-1])

    def pieces(b):
        if b == 1:
            return (OWN - RIM, RIM, 0)
        if b == -1:
            return (0, RIM, RIM + OWN)
        return (0, OWN, RIM)

    def spread(store, which):
        copies = []
        for n, (a, b) in enumerate(around):
            begin, count, place = pieces(b)
            copies.append(send(
                store.at[pl.ds(HERE + begin, count)],
                store.at[pl.ds((1 - a) * BAND + place, count)],
                h_send.at[which, n], h_recv.at[which, n], near(a, b),
            ))
        return copies

    cells = spread(px, 0) + spread(cx, 1)

    def steps_of(w, way):
        return zs // 2 if (w + way) % 2 == 0 else zs // 2 - 1

    ring = {}
    for step in range(1, zs // 2 + 1):
        for w, part in enumerate(parts):
            if step == 1:
                for copy in first[w]:
                    copy.wait_recv()
            for way, d in ((0, 1), (1, -1)):
                if step > 1 and step - 1 <= steps_of(w, way):
                    ring[w, way, step - 1].wait_recv()
                if step <= steps_of(w, way):
                    lines = part.at[lax.rem(z - d * (step - 1) + zs, zs), :, core]
                    ring[w, way, step] = send(
                        lines, lines, z_send.at[w, way, step - 1], z_recv.at[w, way, step - 1], at_z(d)
                    )
                    sent.append(ring[w, way, step])

    cell = lax.broadcasted_iota(jnp.int32, (OWN, EXT), 0)
    other = lax.broadcasted_iota(jnp.int32, (OWN, EXT), 1)
    band = jnp.where(other >= BAND, 1, 0) + jnp.where(other >= 2 * BAND, 1, 0)
    rows = ((other - band * BAND) >> 3) - (cell >> 3)
    cols = (band - 1) * SIDE + (other & 7) - (cell & 7)
    inside = (rows >= 0) & (rows <= 2 * RAD) & (cols >= -RAD) & (cols <= RAD)
    other_row = ((other - band * BAND) >> 3) - RAD + first_row
    cell_row = (cell >> 3) + first_row
    bias[0] = jnp.where(inside & (other_row >= 0) & (other_row < lats), 0.0, -jnp.inf).astype(F32)
    bias[1] = jnp.where(
        inside & (cell_row < lats) & (other_row >= 0) & (other_row < SIDE * lats_dev), 0.0, -jnp.inf
    ).astype(F32)

    def finish(w):
        part = parts[w]
        for way in (0, 1):
            if steps_of(w, way) == zs // 2:
                ring[w, way, zs // 2].wait_recv()
        copy = send(part.at[:, :, core], part.at[:, :, core], s_send.at[w], s_recv.at[w], sibling)
        sent.append(copy)
        return copy

    swaps = [finish(w) for w in range(len(parts))]
    for copy in cells:
        copy.wait_recv()

    scale = 1.0 / math.sqrt(wq.shape[0] // HEADS)
    pairs = HEADS // 2
    bands = [slice(n * BAND, (n + 1) * BAND) for n in range(3)]
    here = slice(HERE, HERE + OWN)

    swaps[0].wait_recv()
    for n, rows_of in enumerate(bands):
        raw = dot_nt(px[rows_of], ge[...].reshape(width, ge.shape[-1]))
        centred = raw - jnp.mean(raw, axis=-1, keepdims=True)
        inverse = lax.rsqrt(jnp.mean(centred * centred, axis=-1, keepdims=True) + EPS)
        normal = centred * inverse
        nx[rows_of] = normal.astype(BF16)
        if n == 1:
            emb[...] = raw[RIM : RIM + OWN]
            nor[...] = normal[RIM : RIM + OWN]
            inv[...] = jnp.broadcast_to(inverse[RIM : RIM + OWN], inv.shape)

    swaps[1].wait_recv()
    ext_row = lax.broadcasted_iota(jnp.int32, (BAND, 1), 0) // SIDE - RAD + first_row
    valid = jnp.where(ext_row < lats, 1.0, 0.0).astype(F32)
    for rows_of in bands:
        grad = dot_nn(cx[rows_of], go[...].reshape(width, go.shape[-1]))
        gx[rows_of] = (grad * valid).astype(BF16)

    for w, weight, result in ((2, wk, kx), (3, wq, qx), (4, wv, vx)):
        swaps[w].wait_recv()

        def order(i, carry, part=parts[w], weight=weight):
            lines = part[i].astype(F32).reshape(8, 2, 8, half)
            begin = pl.ds(pl.multiple_of(i * 64, 64), 64)
            weight[begin, 0:half] = lines[:, 0].reshape(64, half).astype(BF16)
            weight[begin, half:] = lines[:, 1].reshape(64, half).astype(BF16)
            return carry

        lax.fori_loop(0, zs, order, 0)
        for rows_of in bands:
            result[rows_of] = dot_nt(nx[rows_of], weight[...]).astype(BF16)

    low = lax.broadcasted_iota(jnp.int32, (OWN, 128), 1) < 64
    none = jnp.zeros((OWN, 128), BF16)

    def apart(tile):
        return jnp.concatenate([jnp.where(low, tile, none), jnp.where(low, none, tile)], axis=0)

    def together(both):
        return jnp.where(low, both[:OWN], both[OWN:])

    lane = lax.broadcasted_iota(jnp.int32, (OWN, 128), 1)
    known = jnp.zeros((OWN, 128), F32)
    reach = jnp.concatenate([bias[0], bias[0]], axis=0)
    for p in range(pairs):
        tile = slice(p * 128, (p + 1) * 128)
        keys, values = kx[:, tile], vx[:, tile]
        scores = dot_nt(apart(qx[here, tile]), keys) * scale + reach
        top = jnp.max(scores, axis=-1, keepdims=True)
        terms = jnp.exp(scores - top)
        total = jnp.sum(terms, axis=-1, keepdims=True)
        prob = terms / total
        dprob = dot_nt(apart(gx[here, tile]), values)
        delta = jnp.sum(prob * dprob, axis=-1, keepdims=True)
        dscore = (prob * (dprob - delta)).astype(BF16)
        att[:, tile] = together(dot_nn(prob.astype(BF16), values)).astype(BF16)
        dq[:, tile] = together(dot_nn(dscore, keys) * scale).astype(BF16)
        for place, column in ((0, top), (HEADS, total), (2 * HEADS, delta)):
            known = jnp.where(lane == place + 2 * p, column[:OWN], known)
            known = jnp.where(lane == place + 2 * p + 1, column[OWN:], known)

    sx[here] = known
    told = spread(sx, 2)
    mixed = emb[...] + dot_nt(att[...], go[...].reshape(width, go.shape[-1]))
    own_row = lax.broadcasted_iota(jnp.int32, (OWN, 1), 0) // SIDE + first_row
    own_valid = jnp.where(own_row < lats, 1.0, 0.0).astype(F32)
    out_ref[...] = (mixed * own_valid).astype(BF16)
    for copy in told:
        copy.wait_recv()

    facts = jnp.transpose(sx[...], (1, 0))
    reach = jnp.concatenate([bias[1], bias[1]], axis=0)
    for p in range(pairs):
        tile = slice(p * 128, (p + 1) * 128)

        def fact(place):
            first = jnp.broadcast_to(facts[place + 2 * p : place + 2 * p + 1, :EXT], (OWN, EXT))
            second = jnp.broadcast_to(facts[place + 2 * p + 1 : place + 2 * p + 2, :EXT], (OWN, EXT))
            return jnp.concatenate([first, second], axis=0)

        queries, grads = qx[:, tile], gx[:, tile]
        scores = dot_nt(apart(kx[here, tile]), queries) * scale + reach
        prob = jnp.exp(scores - fact(0)) / fact(HEADS)
        dprob = dot_nt(apart(vx[here, tile]), grads)
        dscore = (prob * (dprob - fact(2 * HEADS))).astype(BF16)
        dk[:, tile] = together(dot_nn(dscore, queries) * scale).astype(BF16)
        dv[:, tile] = together(dot_nn(prob.astype(BF16), grads)).astype(BF16)

    slope = dot_nn(dq[...], wq[...]) + dot_nn(dk[...], wk[...]) + dot_nn(dv[...], wv[...])
    normal = nor[...]
    centre = jnp.mean(slope, axis=-1, keepdims=True)
    along = jnp.mean(slope * normal, axis=-1, keepdims=True)
    masked = c_ref[...].astype(F32) * own_valid
    grad_embed = (masked + inv[:, 0:1] * (slope - centre - normal * along)).astype(BF16)
    result = dot_nn(grad_embed, ge[...].reshape(width, ge.shape[-1])).astype(BF16)
    grad_ref[...] = result[:, 0:patch_width]

    for copy in sent + cells + told:
        copy.wait_send()


def body(patches, query_weight, key_weight, value_weight, out_weight, embed_weight, cotangent):
    rows, cols, patch_width = patches.shape
    width = cotangent.shape[-1]
    lons, lats_dev = lax.axis_size("lon"), lax.axis_size("lat")
    zs = lons // 8
    channels = query_weight.shape[1] * lons
    wide_patch = -(-patch_width // 128) * 128
    blocks = (zs, 4, 2, 16)
    vmem = pltpu.VMEM
    dma = pltpu.SemaphoreType.DMA
    out, grad = pl.pallas_call(
        functools.partial(kernel, (lons, lats_dev)),
        out_shape=(
            jax.ShapeDtypeStruct((OWN, width), BF16),
            jax.ShapeDtypeStruct((OWN, patch_width), BF16),
        ),
        in_specs=[pl.BlockSpec(memory_space=vmem)] * 7,
        out_specs=(pl.BlockSpec(memory_space=vmem),) * 2,
        scratch_shapes=[
            vmem(blocks + (wide_patch,), BF16),
            vmem(blocks + (channels,), BF16),
            vmem(blocks + (width // 2,), BF16),
            vmem(blocks + (width // 2,), BF16),
            vmem(blocks + (width // 2,), BF16),
            vmem((channels, width), BF16),
            vmem((channels, width), BF16),
            vmem((channels, width), BF16),
            vmem((EXT, wide_patch), BF16),
            vmem((EXT, width), BF16),
            vmem((512, 128), F32),
            vmem((EXT, width), BF16),
            vmem((EXT, channels), BF16),
            vmem((EXT, channels), BF16),
            vmem((EXT, channels), BF16),
            vmem((EXT, channels), BF16),
            vmem((OWN, width), F32),
            vmem((OWN, width), F32),
            vmem((OWN, 128), F32),
            vmem((OWN, channels), BF16),
            vmem((OWN, channels), BF16),
            vmem((OWN, channels), BF16),
            vmem((OWN, channels), BF16),
            vmem((2, OWN, EXT), F32),
            dma((5, 3)),
            dma((5, 3)),
            dma((5, 2, zs // 2)),
            dma((5, 2, zs // 2)),
            dma((5,)),
            dma((5,)),
            dma((3, 8)),
            dma((3, 8)),
        ],
        compiler_params=pltpu.CompilerParams(
            collective_id=0, has_side_effects=True, vmem_limit_bytes=48 * 1024 * 1024
        ),
    )(
        patches.reshape(rows * cols, patch_width),
        query_weight.T,
        key_weight.T,
        value_weight.T,
        out_weight.T,
        embed_weight.T,
        cotangent.reshape(rows * cols, width),
    )
    return out.reshape(rows, cols, width), grad.reshape(rows, cols, patch_width)


def solution(mesh):
    in_specs = (
        P("lat", "lon", None),
        P(None, "lon"),
        P(None, "lon"),
        P(None, "lon"),
        P(None, "lon"),
        P(None, "lon"),
        P("lat", "lon", None),
    )
    out_specs = (P("lat", "lon", None), P("lat", "lon", None))
    return jax.shard_map(body, mesh=mesh, in_specs=in_specs, out_specs=out_specs, check_vma=False)
```

```python
import functools
import math

import jax
import jax.numpy as jnp
from jax import lax
from jax.experimental import pallas as pl
from jax.experimental.pallas import tpu as pltpu
from jax.sharding import PartitionSpec as P

HEADS = 8
RAD = 6
PAD = 6
EPS = 1e-05
MESH = pl.DeviceIdType.MESH
F32 = jnp.float32
BF16 = jnp.bfloat16

SIDE = 8
OWN = SIDE * SIDE
RIM = RAD * SIDE
BAND = OWN + 2 * RIM
EXT = 3 * BAND
HERE = BAND + RIM

NT = (((1,), (1,)), ((), ()))
NN = (((1,), (0,)), ((), ()))


def dot_nt(left, right):
    return lax.dot_general(left, right, NT, preferred_element_type=F32)


def dot_nn(left, right):
    return lax.dot_general(left, right, NN, preferred_element_type=F32)


WHOLE = ("e",)
SPLIT = ("k", "v", "q", "o")


def kernel(
    sizes, p_ref, q_ref, k_ref, v_ref, o_ref, e_ref, c_ref, out_ref, grad_ref,
    whole, gb, raw8, raw16, rawp, stage, wk, wq, wv, px, cx, sx, nx, qx, kx, vx, gx, emb, nor, inv, att, dq, dk, dv, bias,
    y_send, y_recv, z_send, z_recv, x_send, x_recv, s_send, s_recv, h_send, h_recv, f_send, f_recv, l_sem,
):
    lons, lats_dev = sizes
    lon, lat = lax.axis_index("lon"), lax.axis_index("lat")
    core, yh, z = lax.rem(lon, 2), lax.rem(lon // 2, 4), lon // 8
    x, yl = lat // 2, lax.rem(lat, 2)
    zs, xs = lons // 8, lats_dev // 2
    first_row = lat * SIDE
    lats = SIDE * lats_dev - PAD
    patch_width = p_ref.shape[1]
    width = c_ref.shape[1]
    half = width // 2
    quarter = gb.shape[-1] // xs

    around = [(a, b) for a in (-1, 0, 1) for b in (-1, 0, 1) if (a, b) != (0, 0)]

    def near(a, b):
        return (lax.rem(lon + lons + a, lons), lax.rem(lat + lats_dev + b, lats_dev))

    def at_y(d):
        y = lax.rem(2 * yh + yl + 8 + (2 * yl - 1) * d, 8)
        return ((z * 4 + y // 2) * 2 + core, 2 * x + lax.rem(y, 2))

    def at_z(d):
        return ((lax.rem(z + d + zs, zs) * 4 + yh) * 2 + core, lat)

    def at_x(d):
        return (lon, 2 * lax.rem(x + d + xs, xs) + yl)

    sibling = (lon + 1 - 2 * core, lat)
    greeted = [near(a, b) for a, b in around] + [at_y(1), at_y(2), at_y(-2), at_y(3)]
    greeted += [at_z(1), at_z(-1), at_x(1), at_x(-1), at_x(2), sibling]
    barrier = pltpu.get_barrier_semaphore()
    for partner in greeted:
        pl.semaphore_signal(barrier, inc=1, device_id=partner, device_id_type=MESH)

    here = slice(HERE, HERE + OWN)
    local = [
        pltpu.make_async_copy(source, target, l_sem.at[n])
        for n, (source, target) in enumerate((
            (q_ref, raw8.at[0]), (k_ref, raw8.at[1]), (v_ref, raw8.at[2]),
            (o_ref, raw16), (e_ref, rawp[1]),
            (p_ref, rawp[0]), (c_ref, cx.at[pl.ds(HERE, OWN)]),
        ))
    ]
    for copy in local:
        copy.start()

    for copy in local:
        copy.wait()

    def lanes(d):
        return pl.ds(pl.multiple_of(lax.rem(x + d + xs, xs) * quarter, 128), quarter)

    def folded(n):
        wide = raw8[n].astype(F32)
        return jnp.concatenate([wide[:, :half], wide[:, half:]], axis=0).astype(BF16)

    pads = whole[0].shape[-1]
    whole[0][z, yh, core] = jnp.zeros((16, pads), BF16)
    whole[0][z, yh, core, :, 0:patch_width] = rawp[1][...]
    for n, name in enumerate(SPLIT):
        stage[n] = raw16[...] if name == "o" else folded("qkv".index(name))
    gb[z, yh, core, :, lanes(0)] = stage[x]
    px[here] = jnp.zeros((OWN, px.shape[1]), BF16)
    px[here, 0:patch_width] = rawp[0][...]

    pl.semaphore_wait(barrier, len(greeted))

    sent = []

    def send(source, target, send_sem, recv_sem, partner):
        copy = pltpu.make_async_remote_copy(
            src_ref=source, dst_ref=target, send_sem=send_sem, recv_sem=recv_sem,
            device_id=partner, device_id_type=MESH,
        )
        copy.start()
        sent.append(copy)
        return copy

    order = ("b", 0)
    last = len(order) - 1
    soon = 5

    def lines(part, at):
        return gb.at[at, :, core, :, lanes(0)] if part == "b" else whole[part].at[at, :, core]

    def place_of(way, step):
        return lax.rem(z - (1, -1)[way] * step + zs, zs)

    first = {}
    for i, part in enumerate(order):
        block = gb.at[z, yh, core, :, lanes(0)] if part == "b" else whole[part].at[z, yh, core]
        first[i] = [send(block, block, y_send.at[i, d - 1], y_recv.at[i, d - 1], at_y(d)) for d in (1, 2, 3)]

    def steps_of(i, way):
        return zs // 2 if (way == 1) == (i == last) else zs // 2 - 1

    ring, across, ahead, swap = {}, {}, {}, {}

    def go_across(n, at):
        source = gb.at[at, :, core, :, lanes(0)]
        across[n] = [
            send(source, source, x_send.at[n, side], x_recv.at[n, side], at_x(d)) for side, d in ((0, 1), (1, -1))
        ]
        if n >= soon:
            ahead[n] = send(source, source, x_send.at[n, 2], x_recv.at[n, 2], at_x(2))

    def go_ahead(n, at):
        for copy in across[n]:
            copy.wait_recv()
        if n >= soon:
            return
        d = 1 if n % 2 == 0 else -1
        source = gb.at[at, :, core, :, lanes(-d)]
        ahead[n] = send(source, source, x_send.at[n, 2], x_recv.at[n, 2], at_x(d))

    def go_over(part, n, at):
        if part == "b":
            ahead[n].wait_recv()
        source = gb.at[at, :, core] if part == "b" else whole[part].at[at, :, core]
        i = order.index(part)
        swap[part, n] = send(source, source, s_send.at[i, n], s_recv.at[i, n], sibling)

    def came(step, i):
        if step == 1:
            return [(0, z)]
        return [
            (2 * (step - 1) - 1 + way, place_of(way, step - 1)) for way in (0, 1) if step - 1 <= steps_of(i, way)
        ]

    def numbers(step, i):
        return [(n if step < zs // 2 + 1 else zs - 1, at) for n, at in came(step, i)]

    def arrange(n, at):
        swap["b", n].wait_recv()
        for name, weight in (("k", wk), ("q", wq), ("v", wv)):
            begin_lane = half * SPLIT.index(name)
            wide = gb[at, :, :, :, begin_lane : begin_lane + half].astype(F32).reshape(8, 2, 8, half)
            begin = pl.ds(pl.multiple_of(at * 64, 64), 64)
            weight[begin, 0:half] = wide[:, 0].reshape(64, half).astype(BF16)
            weight[begin, half:] = wide[:, 1].reshape(64, half).astype(BF16)

    def slot(step):
        for i, part in enumerate(order):
            if step <= zs // 2 + 1:
                if step == 1:
                    for copy in first[i]:
                        copy.wait_recv()
                for way in (0, 1):
                    if step > 1 and step - 1 <= steps_of(i, way):
                        ring[i, way, step - 1].wait_recv()
                    if step <= steps_of(i, way):
                        source = lines(part, place_of(way, step - 1))
                        ring[i, way, step] = send(
                            source, source, z_send.at[i, way, step - 1], z_recv.at[i, way, step - 1],
                            at_z((1, -1)[way]),
                        )
                for n, at in numbers(step, i):
                    if part == "b":
                        go_across(n, at)
                    else:
                        go_over(part, n, at)
        if 1 <= step - 1 <= zs // 2 + 1:
            for n, at in numbers(step - 1, 0):
                go_ahead(n, at)
                if n >= soon:
                    go_over("b", n, at)
        if 1 <= step - 2 <= zs // 2 + 1:
            for n, at in numbers(step - 2, 0):
                if n < soon:
                    go_over("b", n, at)
        if 1 <= step - 3 <= zs // 2 + 1:
            for n, at in numbers(step - 3, 0):
                if n < soon:
                    arrange(n, at)

    def arrived(part):
        for n in range(zs):
            swap[part, n].wait_recv()

    slot(1)

    def poleward(store, which):
        return [
            send(store.at[pl.ds(HERE + OWN - RIM, RIM)], store.at[pl.ds(BAND, RIM)],
                 h_send.at[which, 0], h_recv.at[which, 0], near(0, 1)),
            send(store.at[pl.ds(HERE, RIM)], store.at[pl.ds(HERE + OWN, RIM)],
                 h_send.at[which, 1], h_recv.at[which, 1], near(0, -1)),
        ]

    def sideward(store, which):
        source = store.at[pl.ds(BAND, BAND)]
        return [
            send(source, store.at[pl.ds(0, BAND)], h_send.at[which, 2], h_recv.at[which, 2], near(1, 0)),
            send(source, store.at[pl.ds(2 * BAND, BAND)], h_send.at[which, 3], h_recv.at[which, 3], near(-1, 0)),
        ]

    halo = poleward(px, 0), poleward(cx, 1)
    cell = lax.broadcasted_iota(jnp.int32, (OWN, EXT), 0)
    other = lax.broadcasted_iota(jnp.int32, (OWN, EXT), 1)
    band = jnp.where(other >= BAND, 1, 0) + jnp.where(other >= 2 * BAND, 1, 0)
    rows = ((other - band * BAND) >> 3) - (cell >> 3)
    cols = (band - 1) * SIDE + (other & 7) - (cell & 7)
    inside = (rows >= 0) & (rows <= 2 * RAD) & (cols >= -RAD) & (cols <= RAD)
    other_row = ((other - band * BAND) >> 3) - RAD + first_row
    cell_row = (cell >> 3) + first_row
    bias[0] = jnp.where(inside & (other_row >= 0) & (other_row < lats), 0.0, -jnp.inf).astype(F32)
    bias[1] = jnp.where(
        inside & (cell_row < lats) & (other_row >= 0) & (other_row < SIDE * lats_dev), 0.0, -jnp.inf
    ).astype(F32)

    slot(2)
    for copy in halo[0] + halo[1]:
        copy.wait_recv()
    halo = sideward(px, 0), sideward(cx, 1)
    for step in range(3, zs // 2 + 2):
        slot(step)

    def embed(n):
        rows_of = slice(n * BAND, (n + 1) * BAND)
        raw = dot_nt(px[rows_of], whole[0][...].reshape(width, pads))
        centred = raw - jnp.mean(raw, axis=-1, keepdims=True)
        inverse = lax.rsqrt(jnp.mean(centred * centred, axis=-1, keepdims=True) + EPS)
        normal = centred * inverse
        nx[rows_of] = normal.astype(BF16)
        if n == 1:
            emb[...] = raw[RIM : RIM + OWN]
            nor[...] = normal[RIM : RIM + OWN]
            inv[...] = jnp.broadcast_to(inverse[RIM : RIM + OWN], inv.shape)

    bands = [slice(n * BAND, (n + 1) * BAND) for n in range(3)]

    def project(weight, result):
        for rows_of in bands:
            result[rows_of] = dot_nt(nx[rows_of], weight[...]).astype(BF16)

    for copy in halo[0]:
        copy.wait_recv()
    arrived(0)
    embed(0)
    slot(zs // 2 + 2)
    embed(1)
    embed(2)
    slot(zs // 2 + 3)
    for n, at in [(5, place_of(0, 3)), (6, place_of(1, 3)), (zs - 1, place_of(0, 4))]:
        arrange(n, at)
    for weight, result in ((wk, kx), (wq, qx), (wv, vx)):
        project(weight, result)
    at_o = half * SPLIT.index("o")

    def out_rows():
        return gb[:, :, :, :, at_o : at_o + half].reshape(width, half)

    for copy in halo[1]:
        copy.wait_recv()
    ext_row = lax.broadcasted_iota(jnp.int32, (BAND, 1), 0) // SIDE - RAD + first_row
    valid = jnp.where(ext_row < lats, 1.0, 0.0).astype(F32)
    for rows_of in bands:
        gx[rows_of] = (dot_nn(cx[rows_of], out_rows()) * valid).astype(BF16)

    scale = 1.0 / math.sqrt(wq.shape[0] // HEADS)
    pairs = HEADS // 2

    low = lax.broadcasted_iota(jnp.int32, (OWN, 128), 1) < 64
    none = jnp.zeros((OWN, 128), BF16)

    def apart(tile):
        return jnp.concatenate([jnp.where(low, tile, none), jnp.where(low, none, tile)], axis=0)

    def together(both):
        return jnp.where(low, both[:OWN], both[OWN:])

    lane = lax.broadcasted_iota(jnp.int32, (OWN, 128), 1)
    known = jnp.zeros((OWN, 128), F32)
    reach = jnp.concatenate([bias[0], bias[0]], axis=0)
    for p in range(pairs):
        tile = slice(p * 128, (p + 1) * 128)
        keys, values = kx[:, tile], vx[:, tile]
        scores = dot_nt(apart(qx[here, tile]), keys) * scale + reach
        top = jnp.max(scores, axis=-1, keepdims=True)
        terms = jnp.exp(scores - top)
        total = jnp.sum(terms, axis=-1, keepdims=True)
        prob = terms / total
        dprob = dot_nt(apart(gx[here, tile]), values)
        delta = jnp.sum(prob * dprob, axis=-1, keepdims=True)
        dscore = (prob * (dprob - delta)).astype(BF16)
        att[:, tile] = together(dot_nn(prob.astype(BF16), values)).astype(BF16)
        dq[:, tile] = together(dot_nn(dscore, keys) * scale).astype(BF16)
        for place, column in ((0, top), (HEADS, total), (2 * HEADS, delta)):
            known = jnp.where(lane == place + 2 * p, column[:OWN], known)
            known = jnp.where(lane == place + 2 * p + 1, column[OWN:], known)

    sx[here] = known
    told = []
    for n, (a, b) in enumerate(around):
        begin, count, place = {1: (OWN - RIM, RIM, 0), -1: (0, RIM, RIM + OWN), 0: (0, OWN, RIM)}[b]
        told.append(send(
            sx.at[pl.ds(HERE + begin, count)], sx.at[pl.ds((1 - a) * BAND + place, count)],
            f_send.at[n], f_recv.at[n], near(a, b),
        ))
    mixed = emb[...] + dot_nt(att[...], out_rows())
    own_row = lax.broadcasted_iota(jnp.int32, (OWN, 1), 0) // SIDE + first_row
    own_valid = jnp.where(own_row < lats, 1.0, 0.0).astype(F32)
    out_ref[...] = (mixed * own_valid).astype(BF16)
    for copy in told:
        copy.wait_recv()

    facts = jnp.transpose(sx[...], (1, 0))
    reach = jnp.concatenate([bias[1], bias[1]], axis=0)
    for p in range(pairs):
        tile = slice(p * 128, (p + 1) * 128)

        def fact(place):
            first = jnp.broadcast_to(facts[place + 2 * p : place + 2 * p + 1, :EXT], (OWN, EXT))
            second = jnp.broadcast_to(facts[place + 2 * p + 1 : place + 2 * p + 2, :EXT], (OWN, EXT))
            return jnp.concatenate([first, second], axis=0)

        queries, grads = qx[:, tile], gx[:, tile]
        scores = dot_nt(apart(kx[here, tile]), queries) * scale + reach
        prob = jnp.exp(scores - fact(0)) / fact(HEADS)
        dprob = dot_nt(apart(vx[here, tile]), grads)
        dscore = (prob * (dprob - fact(2 * HEADS))).astype(BF16)
        dk[:, tile] = together(dot_nn(dscore, queries) * scale).astype(BF16)
        dv[:, tile] = together(dot_nn(prob.astype(BF16), grads)).astype(BF16)

    slope = dot_nn(dq[...], wq[...]) + dot_nn(dk[...], wk[...]) + dot_nn(dv[...], wv[...])
    normal = nor[...]
    centre = jnp.mean(slope, axis=-1, keepdims=True)
    along = jnp.mean(slope * normal, axis=-1, keepdims=True)
    masked = cx[here].astype(F32) * own_valid
    grad_embed = (masked + inv[:, 0:1] * (slope - centre - normal * along)).astype(BF16)
    result = dot_nn(grad_embed, whole[0][...].reshape(width, pads)).astype(BF16)
    grad_ref[...] = result[:, 0:patch_width]

    for copy in sent:
        copy.wait_send()


def body(patches, query_weight, key_weight, value_weight, out_weight, embed_weight, cotangent):
    rows, cols, patch_width = patches.shape
    width = cotangent.shape[-1]
    lons, lats_dev = lax.axis_size("lon"), lax.axis_size("lat")
    zs = lons // 8
    channels = query_weight.shape[1] * lons
    wide_patch = -(-patch_width // 128) * 128
    blocks = (zs, 4, 2, 16)
    vmem = pltpu.VMEM
    dma = pltpu.SemaphoreType.DMA
    out, grad = pl.pallas_call(
        functools.partial(kernel, (lons, lats_dev)),
        out_shape=(
            jax.ShapeDtypeStruct((OWN, width), BF16),
            jax.ShapeDtypeStruct((OWN, patch_width), BF16),
        ),
        in_specs=[pl.BlockSpec(memory_space=pltpu.HBM)] * 7,
        out_specs=(pl.BlockSpec(memory_space=vmem),) * 2,
        scratch_shapes=[
            [vmem(blocks + (wide_patch if name == "e" else width // 2,), BF16) for name in WHOLE],
            vmem(blocks + (len(SPLIT) * (width // 2),), BF16),
            vmem((3, query_weight.shape[1], width), BF16),
            vmem((width // lons, channels), BF16),
            [vmem((OWN, patch_width), BF16), vmem((width // lons, patch_width), BF16)],
            vmem((len(SPLIT), width // lons, channels), BF16),
            vmem((channels, width), BF16),
            vmem((channels, width), BF16),
            vmem((channels, width), BF16),
            vmem((EXT, wide_patch), BF16),
            vmem((EXT, width), BF16),
            vmem((512, 128), F32),
            vmem((EXT, width), BF16),
            vmem((EXT, channels), BF16),
            vmem((EXT, channels), BF16),
            vmem((EXT, channels), BF16),
            vmem((EXT, channels), BF16),
            vmem((OWN, width), F32),
            vmem((OWN, width), F32),
            vmem((OWN, 128), F32),
            vmem((OWN, channels), BF16),
            vmem((OWN, channels), BF16),
            vmem((OWN, channels), BF16),
            vmem((OWN, channels), BF16),
            vmem((2, OWN, EXT), F32),
            dma((len(WHOLE) + 1, 3)),
            dma((len(WHOLE) + 1, 3)),
            dma((len(WHOLE) + 1, 2, zs // 2)),
            dma((len(WHOLE) + 1, 2, zs // 2)),
            dma((zs, 3)),
            dma((zs, 3)),
            dma((len(WHOLE) + 1, zs)),
            dma((len(WHOLE) + 1, zs)),
            dma((2, 4)),
            dma((2, 4)),
            dma((8,)),
            dma((8,)),
            dma((7,)),
        ],
        compiler_params=pltpu.CompilerParams(
            collective_id=0, has_side_effects=True, vmem_limit_bytes=62 * 1024 * 1024
        ),
    )(
        patches.reshape(rows * cols, patch_width),
        query_weight.T,
        key_weight.T,
        value_weight.T,
        out_weight.T,
        embed_weight.T,
        cotangent.reshape(rows * cols, width),
    )
    return out.reshape(rows, cols, width), grad.reshape(rows, cols, patch_width)


def solution(mesh):
    in_specs = (
        P("lat", "lon", None),
        P(None, "lon"),
        P(None, "lon"),
        P(None, "lon"),
        P(None, "lon"),
        P(None, "lon"),
        P("lat", "lon", None),
    )
    out_specs = (P("lat", "lon", None), P("lat", "lon", None))
    return jax.shard_map(body, mesh=mesh, in_specs=in_specs, out_specs=out_specs, check_vma=False)
```

```python
import functools
import math

import jax
import jax.numpy as jnp
from jax import lax
from jax.experimental import pallas as pl
from jax.experimental.pallas import tpu as pltpu
from jax.sharding import PartitionSpec as P

HEADS = 8
RAD = 6
PAD = 6
EPS = 1e-05
MESH = pl.DeviceIdType.MESH
F32 = jnp.float32
BF16 = jnp.bfloat16

SIDE = 8
OWN = SIDE * SIDE
RIM = RAD * SIDE
BAND = OWN + 2 * RIM
EXT = 3 * BAND
HERE = BAND + RIM

NT = (((1,), (1,)), ((), ()))
NN = (((1,), (0,)), ((), ()))


def dot_nt(left, right):
    return lax.dot_general(left, right, NT, preferred_element_type=F32)


def dot_nn(left, right):
    return lax.dot_general(left, right, NN, preferred_element_type=F32)


WHOLE = ("e",)
SPLIT = ("k", "v", "q", "o")


def kernel(
    sizes, p_ref, q_ref, k_ref, v_ref, o_ref, e_ref, c_ref, out_ref, grad_ref,
    whole, gb, raw8, raw16, rawp, stage, wk, wq, wv, px, cx, sx, nx, qx, kx, vx, gx, emb, nor, inv, att, dq, dk, dv, bias,
    y_send, y_recv, z_send, z_recv, x_send, x_recv, s_send, s_recv, h_send, h_recv, f_send, f_recv, l_sem,
):
    lons, lats_dev = sizes
    lon, lat = lax.axis_index("lon"), lax.axis_index("lat")
    core, yh, z = lax.rem(lon, 2), lax.rem(lon // 2, 4), lon // 8
    x, yl = lat // 2, lax.rem(lat, 2)
    zs, xs = lons // 8, lats_dev // 2
    first_row = lat * SIDE
    lats = SIDE * lats_dev - PAD
    patch_width = p_ref.shape[1]
    width = c_ref.shape[1]
    half = width // 2
    quarter = gb.shape[-1] // xs

    around = [(a, b) for a in (-1, 0, 1) for b in (-1, 0, 1) if (a, b) != (0, 0)]

    def near(a, b):
        return (lax.rem(lon + lons + a, lons), lax.rem(lat + lats_dev + b, lats_dev))

    def at_y(d):
        y = lax.rem(2 * yh + yl + 8 + (2 * yl - 1) * d, 8)
        return ((z * 4 + y // 2) * 2 + core, 2 * x + lax.rem(y, 2))

    def at_z(d):
        return ((lax.rem(z + d + zs, zs) * 4 + yh) * 2 + core, lat)

    def at_x(d):
        return (lon, 2 * lax.rem(x + d + xs, xs) + yl)

    sibling = (lon + 1 - 2 * core, lat)
    greeted = [near(a, b) for a, b in around] + [at_y(1), at_y(2), at_y(-2), at_y(3)]
    greeted += [at_z(1), at_z(-1), at_x(1), at_x(-1), at_x(2), sibling]
    barrier = pltpu.get_barrier_semaphore()
    for partner in greeted:
        pl.semaphore_signal(barrier, inc=1, device_id=partner, device_id_type=MESH)

    here = slice(HERE, HERE + OWN)
    local = [
        pltpu.make_async_copy(source, target, l_sem.at[n])
        for n, (source, target) in enumerate((
            (q_ref, raw8.at[0]), (k_ref, raw8.at[1]), (v_ref, raw8.at[2]),
            (o_ref, raw16), (e_ref, rawp[1]),
            (p_ref, rawp[0]), (c_ref, cx.at[pl.ds(HERE, OWN)]),
        ))
    ]
    for copy in local:
        copy.start()

    for copy in local:
        copy.wait()

    def lanes(d):
        return pl.ds(pl.multiple_of(lax.rem(x + d + xs, xs) * quarter, 128), quarter)

    def folded(n):
        wide = raw8[n].astype(F32)
        return jnp.concatenate([wide[:, :half], wide[:, half:]], axis=0).astype(BF16)

    pads = whole[0].shape[-1]
    whole[0][z, yh, core] = jnp.zeros((16, pads), BF16)
    whole[0][z, yh, core, :, 0:patch_width] = rawp[1][...]
    for n, name in enumerate(SPLIT):
        stage[n] = raw16[...] if name == "o" else folded("qkv".index(name))
    gb[z, yh, core, :, lanes(0)] = stage[x]
    px[here] = jnp.zeros((OWN, px.shape[1]), BF16)
    px[here, 0:patch_width] = rawp[0][...]

    pl.semaphore_wait(barrier, len(greeted))

    sent = []

    def send(source, target, send_sem, recv_sem, partner):
        copy = pltpu.make_async_remote_copy(
            src_ref=source, dst_ref=target, send_sem=send_sem, recv_sem=recv_sem,
            device_id=partner, device_id_type=MESH,
        )
        copy.start()
        sent.append(copy)
        return copy

    order = ("b", 0)
    last = len(order) - 1
    soon = 5

    def lines(part, at):
        return gb.at[at, :, core, :, lanes(0)] if part == "b" else whole[part].at[at, :, core]

    def place_of(way, step):
        return lax.rem(z - (1, -1)[way] * step + zs, zs)

    first = {}
    for i, part in enumerate(order):
        block = gb.at[z, yh, core, :, lanes(0)] if part == "b" else whole[part].at[z, yh, core]
        first[i] = [send(block, block, y_send.at[i, d - 1], y_recv.at[i, d - 1], at_y(d)) for d in (1, 2, 3)]

    def steps_of(i, way):
        return zs // 2 if (way == 1) == (i == last) else zs // 2 - 1

    ring, across, ahead, swap = {}, {}, {}, {}

    def go_across(n, at):
        source = gb.at[at, :, core, :, lanes(0)]
        across[n] = [
            send(source, source, x_send.at[n, side], x_recv.at[n, side], at_x(d)) for side, d in ((0, 1), (1, -1))
        ]
        if n >= soon:
            ahead[n] = send(source, source, x_send.at[n, 2], x_recv.at[n, 2], at_x(2))

    def go_ahead(n, at):
        for copy in across[n]:
            copy.wait_recv()
        if n >= soon:
            return
        d = 1 if n % 2 == 0 else -1
        source = gb.at[at, :, core, :, lanes(-d)]
        ahead[n] = send(source, source, x_send.at[n, 2], x_recv.at[n, 2], at_x(d))

    def go_over(part, n, at):
        if part == "b":
            ahead[n].wait_recv()
        source = gb.at[at, :, core] if part == "b" else whole[part].at[at, :, core]
        i = order.index(part)
        swap[part, n] = send(source, source, s_send.at[i, n], s_recv.at[i, n], sibling)

    def came(step, i):
        if step == 1:
            return [(0, z)]
        return [
            (2 * (step - 1) - 1 + way, place_of(way, step - 1)) for way in (0, 1) if step - 1 <= steps_of(i, way)
        ]

    def numbers(step, i):
        return [(n if step < zs // 2 + 1 else zs - 1, at) for n, at in came(step, i)]

    def arrange(n, at):
        swap["b", n].wait_recv()
        for name, weight in (("k", wk), ("q", wq), ("v", wv)):
            begin_lane = half * SPLIT.index(name)
            wide = gb[at, :, :, :, begin_lane : begin_lane + half].astype(F32).reshape(8, 2, 8, half)
            begin = pl.ds(pl.multiple_of(at * 64, 64), 64)
            weight[begin, 0:half] = wide[:, 0].reshape(64, half).astype(BF16)
            weight[begin, half:] = wide[:, 1].reshape(64, half).astype(BF16)

    def slot(step):
        for i, part in enumerate(order):
            if step <= zs // 2 + 1:
                if step == 1:
                    for copy in first[i]:
                        copy.wait_recv()
                for way in (0, 1):
                    if step > 1 and step - 1 <= steps_of(i, way):
                        ring[i, way, step - 1].wait_recv()
                    if step <= steps_of(i, way):
                        source = lines(part, place_of(way, step - 1))
                        ring[i, way, step] = send(
                            source, source, z_send.at[i, way, step - 1], z_recv.at[i, way, step - 1],
                            at_z((1, -1)[way]),
                        )
                for n, at in numbers(step, i):
                    if part == "b":
                        go_across(n, at)
                    else:
                        go_over(part, n, at)
        if 1 <= step - 1 <= zs // 2 + 1:
            for n, at in numbers(step - 1, 0):
                go_ahead(n, at)
                if n >= soon:
                    go_over("b", n, at)
        if 1 <= step - 2 <= zs // 2 + 1:
            for n, at in numbers(step - 2, 0):
                if n < soon:
                    go_over("b", n, at)
        if 1 <= step - 3 <= zs // 2 + 1:
            for n, at in numbers(step - 3, 0):
                if n < soon:
                    arrange(n, at)

    def arrived(part):
        for n in range(zs):
            swap[part, n].wait_recv()

    slot(1)

    def poleward(store, which):
        return [
            send(store.at[pl.ds(HERE + OWN - RIM, RIM)], store.at[pl.ds(BAND, RIM)],
                 h_send.at[which, 0], h_recv.at[which, 0], near(0, 1)),
            send(store.at[pl.ds(HERE, RIM)], store.at[pl.ds(HERE + OWN, RIM)],
                 h_send.at[which, 1], h_recv.at[which, 1], near(0, -1)),
        ]

    def sideward(store, which):
        source = store.at[pl.ds(BAND, BAND)]
        return [
            send(source, store.at[pl.ds(0, BAND)], h_send.at[which, 2], h_recv.at[which, 2], near(1, 0)),
            send(source, store.at[pl.ds(2 * BAND, BAND)], h_send.at[which, 3], h_recv.at[which, 3], near(-1, 0)),
        ]

    halo = poleward(px, 0), poleward(cx, 1)
    cell = lax.broadcasted_iota(jnp.int32, (OWN, EXT), 0)
    other = lax.broadcasted_iota(jnp.int32, (OWN, EXT), 1)
    band = jnp.where(other >= BAND, 1, 0) + jnp.where(other >= 2 * BAND, 1, 0)
    rows = ((other - band * BAND) >> 3) - (cell >> 3)
    cols = (band - 1) * SIDE + (other & 7) - (cell & 7)
    inside = (rows >= 0) & (rows <= 2 * RAD) & (cols >= -RAD) & (cols <= RAD)
    other_row = ((other - band * BAND) >> 3) - RAD + first_row
    cell_row = (cell >> 3) + first_row
    bias[0] = jnp.where(inside & (other_row >= 0) & (other_row < lats), 0.0, -jnp.inf).astype(F32)
    bias[1] = jnp.where(
        inside & (cell_row < lats) & (other_row >= 0) & (other_row < SIDE * lats_dev), 0.0, -jnp.inf
    ).astype(F32)

    slot(2)
    for copy in halo[0] + halo[1]:
        copy.wait_recv()
    halo = sideward(px, 0), sideward(cx, 1)
    for step in range(3, zs // 2 + 2):
        slot(step)

    def embed(n):
        rows_of = slice(n * BAND, (n + 1) * BAND)
        raw = dot_nt(px[rows_of], whole[0][...].reshape(width, pads))
        centred = raw - jnp.mean(raw, axis=-1, keepdims=True)
        inverse = lax.rsqrt(jnp.mean(centred * centred, axis=-1, keepdims=True) + EPS)
        normal = centred * inverse
        nx[rows_of] = normal.astype(BF16)
        if n == 1:
            emb[...] = raw[RIM : RIM + OWN]
            nor[...] = normal[RIM : RIM + OWN]
            inv[...] = jnp.broadcast_to(inverse[RIM : RIM + OWN], inv.shape)

    def project(weight, result):
        result[...] = dot_nt(nx[...], weight[...]).astype(BF16)

    for copy in halo[0]:
        copy.wait_recv()
    arrived(0)
    embed(0)
    slot(zs // 2 + 2)
    embed(1)
    embed(2)
    slot(zs // 2 + 3)
    for n, at in [(5, place_of(0, 3)), (6, place_of(1, 3)), (zs - 1, place_of(0, 4))]:
        arrange(n, at)
    for weight, result in ((wk, kx), (wq, qx), (wv, vx)):
        project(weight, result)
    at_o = half * SPLIT.index("o")

    def out_rows():
        return gb[:, :, :, :, at_o : at_o + half].reshape(width, half)

    for copy in halo[1]:
        copy.wait_recv()
    ext_row = lax.broadcasted_iota(jnp.int32, (BAND, 1), 0) // SIDE - RAD + first_row
    valid = jnp.where(ext_row < lats, 1.0, 0.0).astype(F32)
    gx[...] = (dot_nn(cx[...], out_rows()) * jnp.concatenate([valid] * 3, axis=0)).astype(BF16)

    scale = 1.0 / math.sqrt(wq.shape[0] // HEADS)
    pairs = HEADS // 2

    low = lax.broadcasted_iota(jnp.int32, (OWN, 128), 1) < 64
    none = jnp.zeros((OWN, 128), BF16)

    def apart(tile):
        return jnp.concatenate([jnp.where(low, tile, none), jnp.where(low, none, tile)], axis=0)

    def together(both):
        return jnp.where(low, both[:OWN], both[OWN:])

    lane = lax.broadcasted_iota(jnp.int32, (OWN, 128), 1)
    known = jnp.zeros((OWN, 128), F32)
    reach = jnp.concatenate([bias[0], bias[0]], axis=0)
    for p in range(pairs):
        tile = slice(p * 128, (p + 1) * 128)
        keys, values = kx[:, tile], vx[:, tile]
        scores = dot_nt(apart(qx[here, tile]), keys) * scale + reach
        top = jnp.max(scores, axis=-1, keepdims=True)
        terms = jnp.exp(scores - top)
        total = jnp.sum(terms, axis=-1, keepdims=True)
        prob = terms / total
        dprob = dot_nt(apart(gx[here, tile]), values)
        delta = jnp.sum(prob * dprob, axis=-1, keepdims=True)
        dscore = (prob * (dprob - delta)).astype(BF16)
        att[:, tile] = together(dot_nn(prob.astype(BF16), values)).astype(BF16)
        dq[:, tile] = together(dot_nn(dscore, keys) * scale).astype(BF16)
        for place, column in ((0, top), (HEADS, total), (2 * HEADS, delta)):
            known = jnp.where(lane == place + 2 * p, column[:OWN], known)
            known = jnp.where(lane == place + 2 * p + 1, column[OWN:], known)

    turned = jnp.transpose(jnp.concatenate([known, jnp.zeros((OWN, 128), F32)], axis=0), (1, 0))
    sx[len(around)] = turned[: 3 * HEADS]
    told = [
        send(sx.at[len(around)], sx.at[n], f_send.at[n], f_recv.at[n], near(a, b)) for n, (a, b) in enumerate(around)
    ]
    mixed = emb[...] + dot_nt(att[...], out_rows())
    own_row = lax.broadcasted_iota(jnp.int32, (OWN, 1), 0) // SIDE + first_row
    own_valid = jnp.where(own_row < lats, 1.0, 0.0).astype(F32)
    out_ref[...] = (mixed * own_valid).astype(BF16)
    for copy in told:
        copy.wait_recv()

    strips = []
    for a in (-1, 0, 1):
        for b in (-1, 0, 1):
            n = len(around) if (a, b) == (0, 0) else around.index((-a, -b))
            begin, end = {-1: (OWN - RIM, OWN), 0: (0, OWN), 1: (0, RIM)}[b]
            strips.append(sx[n][:, begin:end])
    facts = jnp.concatenate(strips, axis=1)
    reach = jnp.concatenate([bias[1], bias[1]], axis=0)
    for p in range(pairs):
        tile = slice(p * 128, (p + 1) * 128)

        def fact(place):
            first = jnp.broadcast_to(facts[place + 2 * p : place + 2 * p + 1, :EXT], (OWN, EXT))
            second = jnp.broadcast_to(facts[place + 2 * p + 1 : place + 2 * p + 2, :EXT], (OWN, EXT))
            return jnp.concatenate([first, second], axis=0)

        queries, grads = qx[:, tile], gx[:, tile]
        scores = dot_nt(apart(kx[here, tile]), queries) * scale + reach
        prob = jnp.exp(scores - fact(0)) / fact(HEADS)
        dprob = dot_nt(apart(vx[here, tile]), grads)
        dscore = (prob * (dprob - fact(2 * HEADS))).astype(BF16)
        dk[:, tile] = together(dot_nn(dscore, queries) * scale).astype(BF16)
        dv[:, tile] = together(dot_nn(prob.astype(BF16), grads)).astype(BF16)

    slope = dot_nn(dq[...], wq[...]) + dot_nn(dk[...], wk[...]) + dot_nn(dv[...], wv[...])
    normal = nor[...]
    centre = jnp.mean(slope, axis=-1, keepdims=True)
    along = jnp.mean(slope * normal, axis=-1, keepdims=True)
    masked = cx[here].astype(F32) * own_valid
    grad_embed = (masked + inv[:, 0:1] * (slope - centre - normal * along)).astype(BF16)
    result = dot_nn(grad_embed, whole[0][...].reshape(width, pads)).astype(BF16)
    grad_ref[...] = result[:, 0:patch_width]

    for copy in sent:
        copy.wait_send()


def body(patches, query_weight, key_weight, value_weight, out_weight, embed_weight, cotangent):
    rows, cols, patch_width = patches.shape
    width = cotangent.shape[-1]
    lons, lats_dev = lax.axis_size("lon"), lax.axis_size("lat")
    zs = lons // 8
    channels = query_weight.shape[1] * lons
    wide_patch = -(-patch_width // 128) * 128
    blocks = (zs, 4, 2, 16)
    vmem = pltpu.VMEM
    dma = pltpu.SemaphoreType.DMA
    out, grad = pl.pallas_call(
        functools.partial(kernel, (lons, lats_dev)),
        out_shape=(
            jax.ShapeDtypeStruct((OWN, width), BF16),
            jax.ShapeDtypeStruct((OWN, patch_width), BF16),
        ),
        in_specs=[pl.BlockSpec(memory_space=pltpu.HBM)] * 7,
        out_specs=(pl.BlockSpec(memory_space=vmem),) * 2,
        scratch_shapes=[
            [vmem(blocks + (wide_patch if name == "e" else width // 2,), BF16) for name in WHOLE],
            vmem(blocks + (len(SPLIT) * (width // 2),), BF16),
            vmem((3, query_weight.shape[1], width), BF16),
            vmem((width // lons, channels), BF16),
            [vmem((OWN, patch_width), BF16), vmem((width // lons, patch_width), BF16)],
            vmem((len(SPLIT), width // lons, channels), BF16),
            vmem((channels, width), BF16),
            vmem((channels, width), BF16),
            vmem((channels, width), BF16),
            vmem((EXT, wide_patch), BF16),
            vmem((EXT, width), BF16),
            vmem((9, 3 * HEADS, 128), F32),
            vmem((EXT, width), BF16),
            vmem((EXT, channels), BF16),
            vmem((EXT, channels), BF16),
            vmem((EXT, channels), BF16),
            vmem((EXT, channels), BF16),
            vmem((OWN, width), F32),
            vmem((OWN, width), F32),
            vmem((OWN, 128), F32),
            vmem((OWN, channels), BF16),
            vmem((OWN, channels), BF16),
            vmem((OWN, channels), BF16),
            vmem((OWN, channels), BF16),
            vmem((2, OWN, EXT), F32),
            dma((len(WHOLE) + 1, 3)),
            dma((len(WHOLE) + 1, 3)),
            dma((len(WHOLE) + 1, 2, zs // 2)),
            dma((len(WHOLE) + 1, 2, zs // 2)),
            dma((zs, 3)),
            dma((zs, 3)),
            dma((len(WHOLE) + 1, zs)),
            dma((len(WHOLE) + 1, zs)),
            dma((2, 4)),
            dma((2, 4)),
            dma((8,)),
            dma((8,)),
            dma((7,)),
        ],
        compiler_params=pltpu.CompilerParams(
            collective_id=0, has_side_effects=True, vmem_limit_bytes=62 * 1024 * 1024
        ),
    )(
        patches.reshape(rows * cols, patch_width),
        query_weight.T,
        key_weight.T,
        value_weight.T,
        out_weight.T,
        embed_weight.T,
        cotangent.reshape(rows * cols, width),
    )
    return out.reshape(rows, cols, width), grad.reshape(rows, cols, patch_width)


def solution(mesh):
    in_specs = (
        P("lat", "lon", None),
        P(None, "lon"),
        P(None, "lon"),
        P(None, "lon"),
        P(None, "lon"),
        P(None, "lon"),
        P("lat", "lon", None),
    )
    out_specs = (P("lat", "lon", None), P("lat", "lon", None))
    return jax.shard_map(body, mesh=mesh, in_specs=in_specs, out_specs=out_specs, check_vma=False)
```

```python
import functools
import math

import jax
import jax.numpy as jnp
from jax import lax
from jax.experimental import pallas as pl
from jax.experimental.pallas import tpu as pltpu
from jax.sharding import PartitionSpec as P

HEADS = 8
RAD = 6
PAD = 6
EPS = 1e-05
MESH = pl.DeviceIdType.MESH
F32 = jnp.float32
BF16 = jnp.bfloat16

SIDE = 8
OWN = SIDE * SIDE
RIM = RAD * SIDE
BAND = OWN + 2 * RIM
EXT = 3 * BAND
HERE = BAND + RIM

NT = (((1,), (1,)), ((), ()))
NN = (((1,), (0,)), ((), ()))


def dot_nt(left, right):
    return lax.dot_general(left, right, NT, preferred_element_type=F32)


def dot_nn(left, right):
    return lax.dot_general(left, right, NN, preferred_element_type=F32)


WHOLE = ("e",)
SPLIT = ("k", "v", "q", "o")


def kernel(
    sizes, p_ref, q_ref, k_ref, v_ref, o_ref, e_ref, c_ref, out_ref, grad_ref,
    whole, gb, raw8, raw16, rawp, stage, wk, wq, wv, px, cx, sx, nx, qx, kx, vx, gx, emb, nor, inv, att, dq, dk, dv, bias, pb, ds, raw, rise,
    y_send, y_recv, z_send, z_recv, x_send, x_recv, s_send, s_recv, h_send, h_recv, f_send, f_recv, l_sem,
):
    lons, lats_dev = sizes
    lon, lat = lax.axis_index("lon"), lax.axis_index("lat")
    core, yh, z = lax.rem(lon, 2), lax.rem(lon // 2, 4), lon // 8
    x, yl = lat // 2, lax.rem(lat, 2)
    zs, xs = lons // 8, lats_dev // 2
    first_row = lat * SIDE
    lats = SIDE * lats_dev - PAD
    patch_width = p_ref.shape[1]
    width = c_ref.shape[1]
    half = width // 2
    quarter = gb.shape[-1] // xs

    around = [(a, b) for a in (-1, 0, 1) for b in (-1, 0, 1) if (a, b) != (0, 0)]

    def near(a, b):
        return (lax.rem(lon + lons + a, lons), lax.rem(lat + lats_dev + b, lats_dev))

    def at_y(d):
        y = lax.rem(2 * yh + yl + 8 + (2 * yl - 1) * d, 8)
        return ((z * 4 + y // 2) * 2 + core, 2 * x + lax.rem(y, 2))

    def at_z(d):
        return ((lax.rem(z + d + zs, zs) * 4 + yh) * 2 + core, lat)

    def at_x(d):
        return (lon, 2 * lax.rem(x + d + xs, xs) + yl)

    sibling = (lon + 1 - 2 * core, lat)
    greeted = [near(a, b) for a, b in around] + [at_y(1), at_y(2), at_y(-2), at_y(3)]
    greeted += [at_z(1), at_z(-1), at_x(1), at_x(-1), at_x(2), sibling]
    barrier = pltpu.get_barrier_semaphore()
    for partner in greeted:
        pl.semaphore_signal(barrier, inc=1, device_id=partner, device_id_type=MESH)

    here = slice(HERE, HERE + OWN)
    local = [
        pltpu.make_async_copy(source, target, l_sem.at[n])
        for n, (source, target) in enumerate((
            (q_ref, raw8.at[0]), (k_ref, raw8.at[1]), (v_ref, raw8.at[2]),
            (o_ref, raw16), (e_ref, rawp[1]),
            (p_ref, rawp[0]), (c_ref, cx.at[pl.ds(HERE, OWN)]),
        ))
    ]
    for copy in local:
        copy.start()

    for copy in local:
        copy.wait()

    def lanes(d):
        return pl.ds(pl.multiple_of(lax.rem(x + d + xs, xs) * quarter, 128), quarter)

    def folded(n):
        wide = raw8[n].astype(F32)
        return jnp.concatenate([wide[:, :half], wide[:, half:]], axis=0).astype(BF16)

    pads = whole[0].shape[-1]
    whole[0][z, yh, core] = jnp.zeros((16, pads), BF16)
    whole[0][z, yh, core, :, 0:patch_width] = rawp[1][...]
    for n, name in enumerate(SPLIT):
        stage[n] = raw16[...] if name == "o" else folded("qkv".index(name))
    gb[z, yh, core, :, lanes(0)] = stage[x]
    px[here] = jnp.zeros((OWN, px.shape[1]), BF16)
    px[here, 0:patch_width] = rawp[0][...]

    pl.semaphore_wait(barrier, len(greeted))

    sent = []

    def send(source, target, send_sem, recv_sem, partner):
        copy = pltpu.make_async_remote_copy(
            src_ref=source, dst_ref=target, send_sem=send_sem, recv_sem=recv_sem,
            device_id=partner, device_id_type=MESH,
        )
        copy.start()
        sent.append(copy)
        return copy

    order = ("b", 0)
    last = len(order) - 1
    soon = 7

    def lines(part, at):
        return gb.at[at, :, core, :, lanes(0)] if part == "b" else whole[part].at[at, :, core]

    def place_of(way, step):
        return lax.rem(z - (1, -1)[way] * step + zs, zs)

    first = {}
    for i, part in enumerate(order):
        block = gb.at[z, yh, core, :, lanes(0)] if part == "b" else whole[part].at[z, yh, core]
        first[i] = [send(block, block, y_send.at[i, d - 1], y_recv.at[i, d - 1], at_y(d)) for d in (1, 2, 3)]

    def steps_of(i, way):
        return zs // 2 if (way == 1) == (i == last) else zs // 2 - 1

    ring, across, ahead, swap = {}, {}, {}, {}

    def go_across(n, at):
        source = gb.at[at, :, core, :, lanes(0)]
        across[n] = [
            send(source, source, x_send.at[n, side], x_recv.at[n, side], at_x(d)) for side, d in ((0, 1), (1, -1))
        ]
        if n >= soon:
            ahead[n] = send(source, source, x_send.at[n, 2], x_recv.at[n, 2], at_x(2))
        go_over("b", n, at)

    def go_ahead(n, at):
        d = 1 if n % 2 == 0 else -1
        across[n][0 if d == 1 else 1].wait_recv()
        if n < soon:
            source = gb.at[at, :, core, :, lanes(-d)]
            ahead[n] = send(source, source, x_send.at[n, 2], x_recv.at[n, 2], at_x(d))
        go_over("b", n, at, -d)
        across[n][1 if d == 1 else 0].wait_recv()
        go_over("b", n, at, d)

    def go_last(n, at):
        ahead[n].wait_recv()
        go_over("b", n, at, 2)

    def go_over(part, n, at, d=0):
        source = gb.at[at, :, core, :, lanes(d)] if part == "b" else whole[part].at[at, :, core]
        i = order.index(part)
        swap[part, n, d] = send(source, source, s_send.at[i, n, d + 1], s_recv.at[i, n, d + 1], sibling)

    def came(step, i):
        if step == 1:
            return [(0, z)]
        return [
            (2 * (step - 1) - 1 + way, place_of(way, step - 1)) for way in (0, 1) if step - 1 <= steps_of(i, way)
        ]

    def numbers(step, i):
        return [(n if step < zs // 2 + 1 else zs - 1, at) for n, at in came(step, i)]

    def arrange(n, at):
        for d in (-1, 0, 1, 2):
            swap["b", n, d].wait_recv()
        for name, weight in (("k", wk), ("q", wq), ("v", wv)):
            begin_lane = half * SPLIT.index(name)
            wide = gb[at, :, :, :, begin_lane : begin_lane + half].astype(F32).reshape(8, 2, 8, half)
            begin = pl.ds(pl.multiple_of(at * 64, 64), 64)
            weight[begin, 0:half] = wide[:, 0].reshape(64, half).astype(BF16)
            weight[begin, half:] = wide[:, 1].reshape(64, half).astype(BF16)

    def slot(step):
        for i, part in enumerate(order):
            if step <= zs // 2 + 1:
                if step == 1:
                    for copy in first[i]:
                        copy.wait_recv()
                for way in (0, 1):
                    if step > 1 and step - 1 <= steps_of(i, way):
                        ring[i, way, step - 1].wait_recv()
                    if step <= steps_of(i, way):
                        source = lines(part, place_of(way, step - 1))
                        ring[i, way, step] = send(
                            source, source, z_send.at[i, way, step - 1], z_recv.at[i, way, step - 1],
                            at_z((1, -1)[way]),
                        )
                for n, at in numbers(step, i):
                    if part == "b":
                        go_across(n, at)
                    else:
                        go_over(part, n, at)
        if 1 <= step - 1 <= zs // 2 + 1:
            for n, at in numbers(step - 1, 0):
                go_ahead(n, at)
                if n >= soon:
                    go_last(n, at)
        if 1 <= step - 2 <= zs // 2 + 1:
            for n, at in numbers(step - 2, 0):
                if n < soon:
                    go_last(n, at)
        if 1 <= step - 3 <= zs // 2 + 1:
            for n, at in numbers(step - 3, 0):
                if n < 5:
                    arrange(n, at)

    slot(1)

    def poleward(store, which):
        return [
            send(store.at[pl.ds(HERE + OWN - RIM, RIM)], store.at[pl.ds(BAND, RIM)],
                 h_send.at[which, 0], h_recv.at[which, 0], near(0, 1)),
            send(store.at[pl.ds(HERE, RIM)], store.at[pl.ds(HERE + OWN, RIM)],
                 h_send.at[which, 1], h_recv.at[which, 1], near(0, -1)),
        ]

    def sideward(store, which):
        source = store.at[pl.ds(BAND, BAND)]
        return [
            send(source, store.at[pl.ds(0, BAND)], h_send.at[which, 2], h_recv.at[which, 2], near(1, 0)),
            send(source, store.at[pl.ds(2 * BAND, BAND)], h_send.at[which, 3], h_recv.at[which, 3], near(-1, 0)),
        ]

    halo = poleward(px, 0), poleward(cx, 1)
    cell = lax.broadcasted_iota(jnp.int32, (OWN, EXT), 0)
    other = lax.broadcasted_iota(jnp.int32, (OWN, EXT), 1)
    band = jnp.where(other >= BAND, 1, 0) + jnp.where(other >= 2 * BAND, 1, 0)
    rows = ((other - band * BAND) >> 3) - (cell >> 3)
    cols = (band - 1) * SIDE + (other & 7) - (cell & 7)
    inside = (rows >= 0) & (rows <= 2 * RAD) & (cols >= -RAD) & (cols <= RAD)
    other_row = ((other - band * BAND) >> 3) - RAD + first_row
    cell_row = (cell >> 3) + first_row
    bias[0] = jnp.where(inside & (other_row >= 0) & (other_row < lats), 0.0, -jnp.inf).astype(F32)
    bias[1] = jnp.where(
        inside & (cell_row < lats) & (other_row >= 0) & (other_row < SIDE * lats_dev), 0.0, -jnp.inf
    ).astype(F32)

    slot(2)
    for copy in halo[0] + halo[1]:
        copy.wait_recv()
    halo = sideward(px, 0), sideward(cx, 1)
    for step in range(3, zs // 2 + 2):
        slot(step)

    def embed(n):
        rows_of = slice(n * BAND, (n + 1) * BAND)
        patch = dot_nt(px[rows_of], whole[0][...].reshape(width, pads))
        centred = patch - jnp.mean(patch, axis=-1, keepdims=True)
        inverse = lax.rsqrt(jnp.mean(centred * centred, axis=-1, keepdims=True) + EPS)
        normal = centred * inverse
        nx[rows_of] = normal.astype(BF16)
        if n == 1:
            emb[...] = patch[RIM : RIM + OWN]
            nor[...] = normal[RIM : RIM + OWN]
            inv[...] = jnp.broadcast_to(inverse[RIM : RIM + OWN], inv.shape)

    def project(weight, result):
        result[...] = dot_nt(nx[...], weight[...]).astype(BF16)

    for copy in halo[0]:
        copy.wait_recv()
    for n in range(zs):
        swap[0, n, 0].wait_recv()
    embed(0)
    slot(zs // 2 + 2)
    embed(1)
    embed(2)
    slot(zs // 2 + 3)
    for n, at in [(5, place_of(0, 3)), (6, place_of(1, 3)), (zs - 1, place_of(0, 4))]:
        arrange(n, at)
    for weight, result in ((wk, kx), (wq, qx), (wv, vx)):
        project(weight, result)
    at_o = half * SPLIT.index("o")

    def out_rows():
        return gb[:, :, :, :, at_o : at_o + half].reshape(width, half)

    for copy in halo[1]:
        copy.wait_recv()
    ext_row = lax.broadcasted_iota(jnp.int32, (BAND, 1), 0) // SIDE - RAD + first_row
    valid = jnp.where(ext_row < lats, 1.0, 0.0).astype(F32)
    gx[...] = (dot_nn(cx[...], out_rows()) * jnp.concatenate([valid] * 3, axis=0)).astype(BF16)

    scale = 1.0 / math.sqrt(wq.shape[0] // HEADS)
    pairs = HEADS // 2

    low = lax.broadcasted_iota(jnp.int32, (OWN, 128), 1) < 64
    none = jnp.zeros((OWN, 128), BF16)

    def apart(tile):
        return jnp.concatenate([jnp.where(low, tile, none), jnp.where(low, none, tile)], axis=0)

    def together(both):
        return jnp.where(low, both[:OWN], both[OWN:])

    lane = lax.broadcasted_iota(jnp.int32, (OWN, 128), 1)
    known = jnp.zeros((OWN, 128), F32)
    reach = jnp.concatenate([bias[0], bias[0]], axis=0)
    for p in range(pairs):
        tile = slice(p * 128, (p + 1) * 128)
        keys, values = kx[:, tile], vx[:, tile]
        scores = dot_nt(apart(qx[here, tile]), keys) * scale + reach
        top = jnp.max(scores, axis=-1, keepdims=True)
        terms = jnp.exp(scores - top)
        total = jnp.sum(terms, axis=-1, keepdims=True)
        prob = terms / total
        dprob = dot_nt(apart(gx[here, tile]), values)
        delta = jnp.sum(prob * dprob, axis=-1, keepdims=True)
        ds[p] = (prob * (dprob - delta)).astype(BF16)
        pb[p] = prob.astype(BF16)
        for place, column in ((0, top), (HEADS, total), (2 * HEADS, delta)):
            known = jnp.where(lane == place + 2 * p, column[:OWN], known)
            known = jnp.where(lane == place + 2 * p + 1, column[OWN:], known)

    turned = jnp.transpose(jnp.concatenate([known, jnp.zeros((OWN, 128), F32)], axis=0), (1, 0))
    sx[len(around)] = turned[: 3 * HEADS]
    told = [
        send(sx.at[len(around)], sx.at[n], f_send.at[n], f_recv.at[n], near(a, b)) for n, (a, b) in enumerate(around)
    ]
    reach = jnp.concatenate([bias[1], bias[1]], axis=0)
    for p in range(pairs):
        tile = slice(p * 128, (p + 1) * 128)
        att[:, tile] = together(dot_nn(pb[p], vx[:, tile])).astype(BF16)
        dq[:, tile] = together(dot_nn(ds[p], kx[:, tile]) * scale).astype(BF16)
        raw[p] = dot_nt(apart(kx[here, tile]), qx[:, tile]) * scale + reach
        rise[p] = dot_nt(apart(vx[here, tile]), gx[:, tile])
    slope_q = dot_nn(dq[...], wq[...])
    mixed = emb[...] + dot_nt(att[...], out_rows())
    own_row = lax.broadcasted_iota(jnp.int32, (OWN, 1), 0) // SIDE + first_row
    own_valid = jnp.where(own_row < lats, 1.0, 0.0).astype(F32)
    out_ref[...] = (mixed * own_valid).astype(BF16)
    for copy in told:
        copy.wait_recv()

    strips = []
    for a in (-1, 0, 1):
        for b in (-1, 0, 1):
            n = len(around) if (a, b) == (0, 0) else around.index((-a, -b))
            begin, end = {-1: (OWN - RIM, OWN), 0: (0, OWN), 1: (0, RIM)}[b]
            strips.append(sx[n][:, begin:end])
    facts = jnp.concatenate(strips, axis=1)
    for p in range(pairs):
        tile = slice(p * 128, (p + 1) * 128)

        def fact(place):
            first = jnp.broadcast_to(facts[place + 2 * p : place + 2 * p + 1, :EXT], (OWN, EXT))
            second = jnp.broadcast_to(facts[place + 2 * p + 1 : place + 2 * p + 2, :EXT], (OWN, EXT))
            return jnp.concatenate([first, second], axis=0)

        queries, grads = qx[:, tile], gx[:, tile]
        prob = jnp.exp(raw[p] - fact(0)) / fact(HEADS)
        dscore = (prob * (rise[p] - fact(2 * HEADS))).astype(BF16)
        dk[:, tile] = together(dot_nn(dscore, queries) * scale).astype(BF16)
        dv[:, tile] = together(dot_nn(prob.astype(BF16), grads)).astype(BF16)

    slope = slope_q + dot_nn(dk[...], wk[...]) + dot_nn(dv[...], wv[...])
    normal = nor[...]
    centre = jnp.mean(slope, axis=-1, keepdims=True)
    along = jnp.mean(slope * normal, axis=-1, keepdims=True)
    masked = cx[here].astype(F32) * own_valid
    grad_embed = (masked + inv[:, 0:1] * (slope - centre - normal * along)).astype(BF16)
    result = dot_nn(grad_embed, whole[0][...].reshape(width, pads)).astype(BF16)
    grad_ref[...] = result[:, 0:patch_width]

    for copy in sent:
        copy.wait_send()


def body(patches, query_weight, key_weight, value_weight, out_weight, embed_weight, cotangent):
    rows, cols, patch_width = patches.shape
    width = cotangent.shape[-1]
    lons, lats_dev = lax.axis_size("lon"), lax.axis_size("lat")
    zs = lons // 8
    channels = query_weight.shape[1] * lons
    wide_patch = -(-patch_width // 128) * 128
    blocks = (zs, 4, 2, 16)
    vmem = pltpu.VMEM
    dma = pltpu.SemaphoreType.DMA
    out, grad = pl.pallas_call(
        functools.partial(kernel, (lons, lats_dev)),
        out_shape=(
            jax.ShapeDtypeStruct((OWN, width), BF16),
            jax.ShapeDtypeStruct((OWN, patch_width), BF16),
        ),
        in_specs=[pl.BlockSpec(memory_space=pltpu.HBM)] * 7,
        out_specs=(pl.BlockSpec(memory_space=vmem),) * 2,
        scratch_shapes=[
            [vmem(blocks + (wide_patch if name == "e" else width // 2,), BF16) for name in WHOLE],
            vmem(blocks + (len(SPLIT) * (width // 2),), BF16),
            vmem((3, query_weight.shape[1], width), BF16),
            vmem((width // lons, channels), BF16),
            [vmem((OWN, patch_width), BF16), vmem((width // lons, patch_width), BF16)],
            vmem((len(SPLIT), width // lons, channels), BF16),
            vmem((channels, width), BF16),
            vmem((channels, width), BF16),
            vmem((channels, width), BF16),
            vmem((EXT, wide_patch), BF16),
            vmem((EXT, width), BF16),
            vmem((9, 3 * HEADS, 128), F32),
            vmem((EXT, width), BF16),
            vmem((EXT, channels), BF16),
            vmem((EXT, channels), BF16),
            vmem((EXT, channels), BF16),
            vmem((EXT, channels), BF16),
            vmem((OWN, width), F32),
            vmem((OWN, width), F32),
            vmem((OWN, 128), F32),
            vmem((OWN, channels), BF16),
            vmem((OWN, channels), BF16),
            vmem((OWN, channels), BF16),
            vmem((OWN, channels), BF16),
            vmem((2, OWN, EXT), F32),
            vmem((HEADS // 2, 2 * OWN, EXT), BF16),
            vmem((HEADS // 2, 2 * OWN, EXT), BF16),
            vmem((HEADS // 2, 2 * OWN, EXT), F32),
            vmem((HEADS // 2, 2 * OWN, EXT), F32),
            dma((len(WHOLE) + 1, 3)),
            dma((len(WHOLE) + 1, 3)),
            dma((len(WHOLE) + 1, 2, zs // 2)),
            dma((len(WHOLE) + 1, 2, zs // 2)),
            dma((zs, 3)),
            dma((zs, 3)),
            dma((len(WHOLE) + 1, zs, 4)),
            dma((len(WHOLE) + 1, zs, 4)),
            dma((2, 4)),
            dma((2, 4)),
            dma((8,)),
            dma((8,)),
            dma((7,)),
        ],
        compiler_params=pltpu.CompilerParams(
            collective_id=0, has_side_effects=True, vmem_limit_bytes=62 * 1024 * 1024
        ),
    )(
        patches.reshape(rows * cols, patch_width),
        query_weight.T,
        key_weight.T,
        value_weight.T,
        out_weight.T,
        embed_weight.T,
        cotangent.reshape(rows * cols, width),
    )
    return out.reshape(rows, cols, width), grad.reshape(rows, cols, patch_width)


def solution(mesh):
    in_specs = (
        P("lat", "lon", None),
        P(None, "lon"),
        P(None, "lon"),
        P(None, "lon"),
        P(None, "lon"),
        P(None, "lon"),
        P("lat", "lon", None),
    )
    out_specs = (P("lat", "lon", None), P("lat", "lon", None))
    return jax.shard_map(body, mesh=mesh, in_specs=in_specs, out_specs=out_specs, check_vma=False)
```

```python
import functools
import math

import jax
import jax.numpy as jnp
from jax import lax
from jax.experimental import pallas as pl
from jax.experimental.pallas import tpu as pltpu
from jax.sharding import PartitionSpec as P

HEADS = 8
RAD = 6
PAD = 6
EPS = 1e-05
MESH = pl.DeviceIdType.MESH
F32 = jnp.float32
BF16 = jnp.bfloat16

SIDE = 8
OWN = SIDE * SIDE
RIM = RAD * SIDE
BAND = OWN + 2 * RIM
EXT = 3 * BAND
HERE = BAND + RIM

NT = (((1,), (1,)), ((), ()))
NN = (((1,), (0,)), ((), ()))


def dot_nt(left, right):
    return lax.dot_general(left, right, NT, preferred_element_type=F32)


def dot_nn(left, right):
    return lax.dot_general(left, right, NN, preferred_element_type=F32)


WHOLE = ("e",)
SPLIT = ("k", "v", "q", "o")


def kernel(
    sizes, p_ref, q_ref, k_ref, v_ref, o_ref, e_ref, c_ref, out_ref, grad_ref,
    whole, gb, raw8, raw16, rawp, stage, wk, wq, wv, px, cx, sx, nx, qx, kx, vx, gx, emb, nor, inv, att, dq, dk, dv, bias, pb, ds, raw, rise,
    y_send, y_recv, z_send, z_recv, x_send, x_recv, s_send, s_recv, h_send, h_recv, f_send, f_recv, l_sem,
):
    lons, lats_dev = sizes
    lon, lat = lax.axis_index("lon"), lax.axis_index("lat")
    core, yh, z = lax.rem(lon, 2), lax.rem(lon // 2, 4), lon // 8
    x, yl = lat // 2, lax.rem(lat, 2)
    zs, xs = lons // 8, lats_dev // 2
    first_row = lat * SIDE
    lats = SIDE * lats_dev - PAD
    patch_width = p_ref.shape[1]
    width = c_ref.shape[1]
    half = width // 2
    quarter = gb.shape[-1] // xs

    around = [(a, b) for a in (-1, 0, 1) for b in (-1, 0, 1) if (a, b) != (0, 0)]

    def near(a, b):
        return (lax.rem(lon + lons + a, lons), lax.rem(lat + lats_dev + b, lats_dev))

    def at_y(d):
        y = lax.rem(2 * yh + yl + 8 + (2 * yl - 1) * d, 8)
        return ((z * 4 + y // 2) * 2 + core, 2 * x + lax.rem(y, 2))

    def at_z(d):
        return ((lax.rem(z + d + zs, zs) * 4 + yh) * 2 + core, lat)

    def at_x(d):
        return (lon, 2 * lax.rem(x + d + xs, xs) + yl)

    sibling = (lon + 1 - 2 * core, lat)
    greeted = [near(a, b) for a, b in around] + [at_y(1), at_y(2), at_y(-2), at_y(3)]
    greeted += [at_z(1), at_z(-1), at_x(1), at_x(-1), at_x(2), sibling]
    barrier = pltpu.get_barrier_semaphore()
    for partner in greeted:
        pl.semaphore_signal(barrier, inc=1, device_id=partner, device_id_type=MESH)

    here = slice(HERE, HERE + OWN)
    local = [
        pltpu.make_async_copy(source, target, l_sem.at[n])
        for n, (source, target) in enumerate((
            (q_ref, raw8.at[0]), (k_ref, raw8.at[1]), (v_ref, raw8.at[2]),
            (o_ref, raw16), (e_ref, rawp[1]),
            (p_ref, rawp[0]), (c_ref, cx.at[pl.ds(HERE, OWN)]),
        ))
    ]
    for copy in local:
        copy.start()

    for copy in local:
        copy.wait()

    def lanes(d):
        return pl.ds(pl.multiple_of(lax.rem(x + d + xs, xs) * quarter, 128), quarter)

    def folded(n):
        wide = raw8[n].astype(F32)
        return jnp.concatenate([wide[:, :half], wide[:, half:]], axis=0).astype(BF16)

    pads = whole[0].shape[-1]
    whole[0][z, yh, core] = jnp.zeros((16, pads), BF16)
    whole[0][z, yh, core, :, 0:patch_width] = rawp[1][...]
    for n, name in enumerate(SPLIT):
        stage[n] = raw16[...] if name == "o" else folded("qkv".index(name))
    gb[z, yh, core, :, lanes(0)] = stage[x]
    px[here] = jnp.zeros((OWN, px.shape[1]), BF16)
    px[here, 0:patch_width] = rawp[0][...]

    pl.semaphore_wait(barrier, len(greeted))

    sent = []

    def send(source, target, send_sem, recv_sem, partner):
        copy = pltpu.make_async_remote_copy(
            src_ref=source, dst_ref=target, send_sem=send_sem, recv_sem=recv_sem,
            device_id=partner, device_id_type=MESH,
        )
        copy.start()
        sent.append(copy)
        return copy

    order = ("b", 0)
    last = len(order) - 1
    soon = 7

    def lines(part, at):
        return gb.at[at, :, core, :, lanes(0)] if part == "b" else whole[part].at[at, :, core]

    def place_of(way, step):
        return lax.rem(z - (1, -1)[way] * step + zs, zs)

    first = {}
    for i, part in enumerate(order):
        block = gb.at[z, yh, core, :, lanes(0)] if part == "b" else whole[part].at[z, yh, core]
        first[i] = [send(block, block, y_send.at[i, d - 1], y_recv.at[i, d - 1], at_y(d)) for d in (1, 2, 3)]

    def steps_of(i, way):
        return zs // 2 if (way == 1) == (i == last) else zs // 2 - 1

    ring, across, ahead, swap = {}, {}, {}, {}

    def go_across(n, at):
        source = gb.at[at, :, core, :, lanes(0)]
        across[n] = [
            send(source, source, x_send.at[n, side], x_recv.at[n, side], at_x(d)) for side, d in ((0, 1), (1, -1))
        ]
        if n >= soon:
            ahead[n] = send(source, source, x_send.at[n, 2], x_recv.at[n, 2], at_x(2))
        go_over("b", n, at)

    def go_ahead(n, at):
        d = 1 if n % 2 == 0 else -1
        across[n][0 if d == 1 else 1].wait_recv()
        if n < soon:
            source = gb.at[at, :, core, :, lanes(-d)]
            ahead[n] = send(source, source, x_send.at[n, 2], x_recv.at[n, 2], at_x(d))
        go_over("b", n, at, -d)
        across[n][1 if d == 1 else 0].wait_recv()
        go_over("b", n, at, d)

    def go_last(n, at):
        ahead[n].wait_recv()
        go_over("b", n, at, 2)

    def go_over(part, n, at, d=0):
        source = gb.at[at, :, core, :, lanes(d)] if part == "b" else whole[part].at[at, :, core]
        i = order.index(part)
        swap[part, n, d] = send(source, source, s_send.at[i, n, d + 1], s_recv.at[i, n, d + 1], sibling)

    def came(step, i):
        if step == 1:
            return [(0, z)]
        return [
            (2 * (step - 1) - 1 + way, place_of(way, step - 1)) for way in (0, 1) if step - 1 <= steps_of(i, way)
        ]

    def numbers(step, i):
        return [(n if step < zs // 2 + 1 else zs - 1, at) for n, at in came(step, i)]

    def arrange(n, at):
        for d in (-1, 0, 1, 2):
            swap["b", n, d].wait_recv()
        for name, weight in (("k", wk), ("q", wq), ("v", wv)):
            begin_lane = half * SPLIT.index(name)
            wide = gb[at, :, :, :, begin_lane : begin_lane + half].astype(F32).reshape(8, 2, 8, half)
            begin = pl.ds(pl.multiple_of(at * 64, 64), 64)
            weight[begin, 0:half] = wide[:, 0].reshape(64, half).astype(BF16)
            weight[begin, half:] = wide[:, 1].reshape(64, half).astype(BF16)

    def slot(step):
        for i, part in enumerate(order):
            if step <= zs // 2 + 1:
                if step == 1:
                    for copy in first[i]:
                        copy.wait_recv()
                for way in (0, 1):
                    if step > 1 and step - 1 <= steps_of(i, way):
                        ring[i, way, step - 1].wait_recv()
                    if step <= steps_of(i, way):
                        source = lines(part, place_of(way, step - 1))
                        ring[i, way, step] = send(
                            source, source, z_send.at[i, way, step - 1], z_recv.at[i, way, step - 1],
                            at_z((1, -1)[way]),
                        )
                for n, at in numbers(step, i):
                    if part == "b":
                        go_across(n, at)
                    else:
                        go_over(part, n, at)
        if 1 <= step - 1 <= zs // 2 + 1:
            for n, at in numbers(step - 1, 0):
                go_ahead(n, at)
                if n >= soon:
                    go_last(n, at)
        if 1 <= step - 2 <= zs // 2 + 1:
            for n, at in numbers(step - 2, 0):
                if n < soon:
                    go_last(n, at)
        if 1 <= step - 3 <= zs // 2 + 1:
            for n, at in numbers(step - 3, 0):
                if n < 5:
                    arrange(n, at)

    slot(1)

    def poleward(store, which):
        return [
            send(store.at[pl.ds(HERE + OWN - RIM, RIM)], store.at[pl.ds(BAND, RIM)],
                 h_send.at[which, 0], h_recv.at[which, 0], near(0, 1)),
            send(store.at[pl.ds(HERE, RIM)], store.at[pl.ds(HERE + OWN, RIM)],
                 h_send.at[which, 1], h_recv.at[which, 1], near(0, -1)),
        ]

    def sideward(store, which):
        source = store.at[pl.ds(BAND, BAND)]
        return [
            send(source, store.at[pl.ds(0, BAND)], h_send.at[which, 2], h_recv.at[which, 2], near(1, 0)),
            send(source, store.at[pl.ds(2 * BAND, BAND)], h_send.at[which, 3], h_recv.at[which, 3], near(-1, 0)),
        ]

    halo = poleward(px, 0), poleward(cx, 1)
    cell = lax.broadcasted_iota(jnp.int32, (OWN, EXT), 0)
    other = lax.broadcasted_iota(jnp.int32, (OWN, EXT), 1)
    band = jnp.where(other >= BAND, 1, 0) + jnp.where(other >= 2 * BAND, 1, 0)
    rows = ((other - band * BAND) >> 3) - (cell >> 3)
    cols = (band - 1) * SIDE + (other & 7) - (cell & 7)
    inside = (rows >= 0) & (rows <= 2 * RAD) & (cols >= -RAD) & (cols <= RAD)
    other_row = ((other - band * BAND) >> 3) - RAD + first_row
    cell_row = (cell >> 3) + first_row
    bias[0] = jnp.where(inside & (other_row >= 0) & (other_row < lats), 0.0, -jnp.inf).astype(F32)
    bias[1] = jnp.where(
        inside & (cell_row < lats) & (other_row >= 0) & (other_row < SIDE * lats_dev), 0.0, -jnp.inf
    ).astype(F32)

    slot(2)
    slot(3)
    for copy in halo[0] + halo[1]:
        copy.wait_recv()
    halo = sideward(px, 0), sideward(cx, 1)
    for step in range(4, zs // 2 + 2):
        slot(step)

    def embed(n):
        rows_of = slice(n * BAND, (n + 1) * BAND)
        patch = dot_nt(px[rows_of], whole[0][...].reshape(width, pads))
        centred = patch - jnp.mean(patch, axis=-1, keepdims=True)
        inverse = lax.rsqrt(jnp.mean(centred * centred, axis=-1, keepdims=True) + EPS)
        normal = centred * inverse
        nx[rows_of] = normal.astype(BF16)
        if n == 1:
            emb[...] = patch[RIM : RIM + OWN]
            nor[...] = normal[RIM : RIM + OWN]
            inv[...] = jnp.broadcast_to(inverse[RIM : RIM + OWN], inv.shape)

    def project(weight, result):
        result[...] = dot_nt(nx[...], weight[...]).astype(BF16)

    for copy in halo[0]:
        copy.wait_recv()
    for n in range(zs):
        swap[0, n, 0].wait_recv()
    embed(0)
    slot(zs // 2 + 2)
    embed(1)
    embed(2)
    slot(zs // 2 + 3)
    for n, at in [(5, place_of(0, 3)), (6, place_of(1, 3)), (zs - 1, place_of(0, 4))]:
        arrange(n, at)
    for weight, result in ((wk, kx), (wq, qx), (wv, vx)):
        project(weight, result)
    at_o = half * SPLIT.index("o")

    def out_rows():
        return gb[:, :, :, :, at_o : at_o + half].reshape(width, half)

    for copy in halo[1]:
        copy.wait_recv()
    ext_row = lax.broadcasted_iota(jnp.int32, (BAND, 1), 0) // SIDE - RAD + first_row
    valid = jnp.where(ext_row < lats, 1.0, 0.0).astype(F32)
    gx[...] = (dot_nn(cx[...], out_rows()) * jnp.concatenate([valid] * 3, axis=0)).astype(BF16)

    scale = 1.0 / math.sqrt(wq.shape[0] // HEADS)
    pairs = HEADS // 2

    low = lax.broadcasted_iota(jnp.int32, (OWN, 128), 1) < 64
    none = jnp.zeros((OWN, 128), BF16)

    def apart(tile):
        return jnp.concatenate([jnp.where(low, tile, none), jnp.where(low, none, tile)], axis=0)

    def together(both):
        return jnp.where(low, both[:OWN], both[OWN:])

    lane = lax.broadcasted_iota(jnp.int32, (OWN, 128), 1)
    known = jnp.zeros((OWN, 128), F32)
    reach = jnp.concatenate([bias[0], bias[0]], axis=0)
    for p in range(pairs):
        tile = slice(p * 128, (p + 1) * 128)
        keys, values = kx[:, tile], vx[:, tile]
        scores = dot_nt(apart(qx[here, tile]), keys) * scale + reach
        top = jnp.max(scores, axis=-1, keepdims=True)
        terms = jnp.exp(scores - top)
        total = jnp.sum(terms, axis=-1, keepdims=True)
        prob = terms / total
        dprob = dot_nt(apart(gx[here, tile]), values)
        delta = jnp.sum(prob * dprob, axis=-1, keepdims=True)
        ds[p] = (prob * (dprob - delta)).astype(BF16)
        pb[p] = prob.astype(BF16)
        for place, column in ((0, top), (HEADS, total), (2 * HEADS, delta)):
            known = jnp.where(lane == place + 2 * p, column[:OWN], known)
            known = jnp.where(lane == place + 2 * p + 1, column[OWN:], known)

    turned = jnp.transpose(jnp.concatenate([known, jnp.zeros((OWN, 128), F32)], axis=0), (1, 0))
    sx[len(around)] = turned[: 3 * HEADS]
    told = [
        send(sx.at[len(around)], sx.at[n], f_send.at[n], f_recv.at[n], near(a, b)) for n, (a, b) in enumerate(around)
    ]
    reach = jnp.concatenate([bias[1], bias[1]], axis=0)
    for p in range(pairs):
        tile = slice(p * 128, (p + 1) * 128)
        att[:, tile] = together(dot_nn(pb[p], vx[:, tile])).astype(BF16)
        dq[:, tile] = together(dot_nn(ds[p], kx[:, tile]) * scale).astype(BF16)
        raw[p] = dot_nt(apart(kx[here, tile]), qx[:, tile]) * scale + reach
        rise[p] = dot_nt(apart(vx[here, tile]), gx[:, tile])
    slope_q = dot_nn(dq[...], wq[...])
    mixed = emb[...] + dot_nt(att[...], out_rows())
    own_row = lax.broadcasted_iota(jnp.int32, (OWN, 1), 0) // SIDE + first_row
    own_valid = jnp.where(own_row < lats, 1.0, 0.0).astype(F32)
    out_ref[...] = (mixed * own_valid).astype(BF16)
    for copy in told:
        copy.wait_recv()

    strips = []
    for a in (-1, 0, 1):
        for b in (-1, 0, 1):
            n = len(around) if (a, b) == (0, 0) else around.index((-a, -b))
            begin, end = {-1: (OWN - RIM, OWN), 0: (0, OWN), 1: (0, RIM)}[b]
            strips.append(sx[n][:, begin:end])
    facts = jnp.concatenate(strips, axis=1)
    for p in range(pairs):
        tile = slice(p * 128, (p + 1) * 128)

        def fact(place):
            first = jnp.broadcast_to(facts[place + 2 * p : place + 2 * p + 1, :EXT], (OWN, EXT))
            second = jnp.broadcast_to(facts[place + 2 * p + 1 : place + 2 * p + 2, :EXT], (OWN, EXT))
            return jnp.concatenate([first, second], axis=0)

        queries, grads = qx[:, tile], gx[:, tile]
        prob = jnp.exp(raw[p] - fact(0)) / fact(HEADS)
        dscore = (prob * (rise[p] - fact(2 * HEADS))).astype(BF16)
        dk[:, tile] = together(dot_nn(dscore, queries) * scale).astype(BF16)
        dv[:, tile] = together(dot_nn(prob.astype(BF16), grads)).astype(BF16)

    slope = slope_q + dot_nn(dk[...], wk[...]) + dot_nn(dv[...], wv[...])
    normal = nor[...]
    centre = jnp.mean(slope, axis=-1, keepdims=True)
    along = jnp.mean(slope * normal, axis=-1, keepdims=True)
    masked = cx[here].astype(F32) * own_valid
    grad_embed = (masked + inv[:, 0:1] * (slope - centre - normal * along)).astype(BF16)
    result = dot_nn(grad_embed, whole[0][...].reshape(width, pads)).astype(BF16)
    grad_ref[...] = result[:, 0:patch_width]

    for copy in sent:
        copy.wait_send()


def body(patches, query_weight, key_weight, value_weight, out_weight, embed_weight, cotangent):
    rows, cols, patch_width = patches.shape
    width = cotangent.shape[-1]
    lons, lats_dev = lax.axis_size("lon"), lax.axis_size("lat")
    zs = lons // 8
    channels = query_weight.shape[1] * lons
    wide_patch = -(-patch_width // 128) * 128
    blocks = (zs, 4, 2, 16)
    vmem = pltpu.VMEM
    dma = pltpu.SemaphoreType.DMA
    out, grad = pl.pallas_call(
        functools.partial(kernel, (lons, lats_dev)),
        out_shape=(
            jax.ShapeDtypeStruct((OWN, width), BF16),
            jax.ShapeDtypeStruct((OWN, patch_width), BF16),
        ),
        in_specs=[pl.BlockSpec(memory_space=pltpu.HBM)] * 7,
        out_specs=(pl.BlockSpec(memory_space=vmem),) * 2,
        scratch_shapes=[
            [vmem(blocks + (wide_patch if name == "e" else width // 2,), BF16) for name in WHOLE],
            vmem(blocks + (len(SPLIT) * (width // 2),), BF16),
            vmem((3, query_weight.shape[1], width), BF16),
            vmem((width // lons, channels), BF16),
            [vmem((OWN, patch_width), BF16), vmem((width // lons, patch_width), BF16)],
            vmem((len(SPLIT), width // lons, channels), BF16),
            vmem((channels, width), BF16),
            vmem((channels, width), BF16),
            vmem((channels, width), BF16),
            vmem((EXT, wide_patch), BF16),
            vmem((EXT, width), BF16),
            vmem((9, 3 * HEADS, 128), F32),
            vmem((EXT, width), BF16),
            vmem((EXT, channels), BF16),
            vmem((EXT, channels), BF16),
            vmem((EXT, channels), BF16),
            vmem((EXT, channels), BF16),
            vmem((OWN, width), F32),
            vmem((OWN, width), F32),
            vmem((OWN, 128), F32),
            vmem((OWN, channels), BF16),
            vmem((OWN, channels), BF16),
            vmem((OWN, channels), BF16),
            vmem((OWN, channels), BF16),
            vmem((2, OWN, EXT), F32),
            vmem((HEADS // 2, 2 * OWN, EXT), BF16),
            vmem((HEADS // 2, 2 * OWN, EXT), BF16),
            vmem((HEADS // 2, 2 * OWN, EXT), F32),
            vmem((HEADS // 2, 2 * OWN, EXT), F32),
            dma((len(WHOLE) + 1, 3)),
            dma((len(WHOLE) + 1, 3)),
            dma((len(WHOLE) + 1, 2, zs // 2)),
            dma((len(WHOLE) + 1, 2, zs // 2)),
            dma((zs, 3)),
            dma((zs, 3)),
            dma((len(WHOLE) + 1, zs, 4)),
            dma((len(WHOLE) + 1, zs, 4)),
            dma((2, 4)),
            dma((2, 4)),
            dma((8,)),
            dma((8,)),
            dma((7,)),
        ],
        compiler_params=pltpu.CompilerParams(
            collective_id=0, has_side_effects=True, vmem_limit_bytes=62 * 1024 * 1024
        ),
    )(
        patches.reshape(rows * cols, patch_width),
        query_weight.T,
        key_weight.T,
        value_weight.T,
        out_weight.T,
        embed_weight.T,
        cotangent.reshape(rows * cols, width),
    )
    return out.reshape(rows, cols, width), grad.reshape(rows, cols, patch_width)


def solution(mesh):
    in_specs = (
        P("lat", "lon", None),
        P(None, "lon"),
        P(None, "lon"),
        P(None, "lon"),
        P(None, "lon"),
        P(None, "lon"),
        P("lat", "lon", None),
    )
    out_specs = (P("lat", "lon", None), P("lat", "lon", None))
    return jax.shard_map(body, mesh=mesh, in_specs=in_specs, out_specs=out_specs, check_vma=False)
```

```python
import functools
import math

import jax
import jax.numpy as jnp
from jax import lax
from jax.experimental import pallas as pl
from jax.experimental.pallas import tpu as pltpu
from jax.sharding import PartitionSpec as P

HEADS = 8
RAD = 6
PAD = 6
EPS = 1e-05
MESH = pl.DeviceIdType.MESH
F32 = jnp.float32
BF16 = jnp.bfloat16

SIDE = 8
OWN = SIDE * SIDE
RIM = RAD * SIDE
BAND = OWN + 2 * RIM
EXT = 3 * BAND
HERE = BAND + RIM

NT = (((1,), (1,)), ((), ()))
NN = (((1,), (0,)), ((), ()))


def dot_nt(left, right):
    return lax.dot_general(left, right, NT, preferred_element_type=F32)


def dot_nn(left, right):
    return lax.dot_general(left, right, NN, preferred_element_type=F32)


WHOLE = ("e",)
SPLIT = ("k", "v", "q", "o")


def kernel(
    sizes, p_ref, q_ref, k_ref, v_ref, o_ref, e_ref, c_ref, out_ref, grad_ref,
    whole, gb, raw8, raw16, rawp, stage, wk, wq, wv, px, cx, sx, nx, qx, kx, vx, gx, emb, nor, inv, att, dq, dk, dv, bias, pb, ds, raw, rise,
    y_send, y_recv, z_send, z_recv, x_send, x_recv, s_send, s_recv, h_send, h_recv, f_send, f_recv, l_sem,
):
    lons, lats_dev = sizes
    lon, lat = lax.axis_index("lon"), lax.axis_index("lat")
    core, yh, z = lax.rem(lon, 2), lax.rem(lon // 2, 4), lon // 8
    x, yl = lat // 2, lax.rem(lat, 2)
    zs, xs = lons // 8, lats_dev // 2
    first_row = lat * SIDE
    lats = SIDE * lats_dev - PAD
    patch_width = p_ref.shape[1]
    width = c_ref.shape[1]
    half = width // 2
    quarter = gb.shape[-1] // xs

    around = [(a, b) for a in (-1, 0, 1) for b in (-1, 0, 1) if (a, b) != (0, 0)]

    def near(a, b):
        return (lax.rem(lon + lons + a, lons), lax.rem(lat + lats_dev + b, lats_dev))

    def at_y(d):
        y = lax.rem(2 * yh + yl + 8 + (2 * yl - 1) * d, 8)
        return ((z * 4 + y // 2) * 2 + core, 2 * x + lax.rem(y, 2))

    def at_z(d):
        return ((lax.rem(z + d + zs, zs) * 4 + yh) * 2 + core, lat)

    def at_x(d):
        return (lon, 2 * lax.rem(x + d + xs, xs) + yl)

    sibling = (lon + 1 - 2 * core, lat)
    greeted = [near(a, b) for a, b in around] + [at_y(1), at_y(2), at_y(-2), at_y(3)]
    greeted += [at_z(1), at_z(-1), at_x(1), at_x(-1), at_x(2), sibling]
    barrier = pltpu.get_barrier_semaphore()
    for partner in greeted:
        pl.semaphore_signal(barrier, inc=1, device_id=partner, device_id_type=MESH)

    here = slice(HERE, HERE + OWN)
    local = [
        pltpu.make_async_copy(source, target, l_sem.at[n])
        for n, (source, target) in enumerate((
            (q_ref, raw8.at[0]), (k_ref, raw8.at[1]), (v_ref, raw8.at[2]),
            (o_ref, raw16), (e_ref, rawp[1]),
            (p_ref, rawp[0]), (c_ref, cx.at[pl.ds(HERE, OWN)]),
        ))
    ]
    for copy in local:
        copy.start()

    for copy in local:
        copy.wait()

    def lanes(d):
        return pl.ds(pl.multiple_of(lax.rem(x + d + xs, xs) * quarter, 128), quarter)

    def folded(n):
        wide = raw8[n].astype(F32)
        return jnp.concatenate([wide[:, :half], wide[:, half:]], axis=0).astype(BF16)

    pads = whole[0].shape[-1]
    whole[0][z, yh, core] = jnp.zeros((16, pads), BF16)
    whole[0][z, yh, core, :, 0:patch_width] = rawp[1][...]
    for n, name in enumerate(SPLIT):
        stage[n] = raw16[...] if name == "o" else folded("qkv".index(name))
    gb[z, yh, core, :, lanes(0)] = stage[x]
    px[here] = jnp.zeros((OWN, px.shape[1]), BF16)
    px[here, 0:patch_width] = rawp[0][...]

    pl.semaphore_wait(barrier, len(greeted))

    sent = []

    def send(source, target, send_sem, recv_sem, partner):
        copy = pltpu.make_async_remote_copy(
            src_ref=source, dst_ref=target, send_sem=send_sem, recv_sem=recv_sem,
            device_id=partner, device_id_type=MESH,
        )
        copy.start()
        sent.append(copy)
        return copy

    order = ("b", 0)
    last = len(order) - 1
    soon = 7

    def lines(part, at):
        return gb.at[at, :, core, :, lanes(0)] if part == "b" else whole[part].at[at, :, core]

    def place_of(way, step):
        return lax.rem(z - (1, -1)[way] * step + zs, zs)

    first = {}
    for i, part in enumerate(order):
        block = gb.at[z, yh, core, :, lanes(0)] if part == "b" else whole[part].at[z, yh, core]
        first[i] = [send(block, block, y_send.at[i, d - 1], y_recv.at[i, d - 1], at_y(d)) for d in (1, 2, 3)]

    def steps_of(i, way):
        return zs // 2 if (way == 1) == (i == last) else zs // 2 - 1

    ring, across, ahead, swap = {}, {}, {}, {}

    def go_across(n, at):
        source = gb.at[at, :, core, :, lanes(0)]
        across[n] = [
            send(source, source, x_send.at[n, side], x_recv.at[n, side], at_x(d)) for side, d in ((0, 1), (1, -1))
        ]
        if n >= soon:
            ahead[n] = send(source, source, x_send.at[n, 2], x_recv.at[n, 2], at_x(2))
        go_over("b", n, at)

    def go_ahead(n, at):
        d = 1 if n % 2 == 0 else -1
        across[n][0 if d == 1 else 1].wait_recv()
        if n < soon:
            source = gb.at[at, :, core, :, lanes(-d)]
            ahead[n] = send(source, source, x_send.at[n, 2], x_recv.at[n, 2], at_x(d))
        go_over("b", n, at, -d)
        across[n][1 if d == 1 else 0].wait_recv()
        go_over("b", n, at, d)

    def go_last(n, at):
        ahead[n].wait_recv()
        go_over("b", n, at, 2)

    def go_over(part, n, at, d=0):
        source = gb.at[at, :, core, :, lanes(d)] if part == "b" else whole[part].at[at, :, core]
        i = order.index(part)
        swap[part, n, d] = send(source, source, s_send.at[i, n, d + 1], s_recv.at[i, n, d + 1], sibling)

    def came(step, i):
        if step == 1:
            return [(0, z)]
        return [
            (2 * (step - 1) - 1 + way, place_of(way, step - 1)) for way in (0, 1) if step - 1 <= steps_of(i, way)
        ]

    def numbers(step, i):
        return [(n if step < zs // 2 + 1 else zs - 1, at) for n, at in came(step, i)]

    def arrange(n, at):
        for d in (-1, 0, 1, 2):
            swap["b", n, d].wait_recv()
        for name, weight in (("k", wk), ("q", wq), ("v", wv)):
            begin_lane = half * SPLIT.index(name)
            wide = gb[at, :, :, :, begin_lane : begin_lane + half].astype(F32).reshape(8, 2, 8, half)
            begin = pl.ds(pl.multiple_of(at * 64, 64), 64)
            weight[begin, 0:half] = wide[:, 0].reshape(64, half).astype(BF16)
            weight[begin, half:] = wide[:, 1].reshape(64, half).astype(BF16)

    def hand_on(step):
        if 1 <= step - 1 <= zs // 2 + 1:
            for n, at in numbers(step - 1, 0):
                go_ahead(n, at)
                if n >= soon:
                    go_last(n, at)
        if 1 <= step - 2 <= zs // 2 + 1:
            for n, at in numbers(step - 2, 0):
                if n < soon:
                    go_last(n, at)

    def slot(step):
        for i, part in enumerate(order):
            if i == 1:
                hand_on(step)
            if step <= zs // 2 + 1:
                if step == 1:
                    for copy in first[i]:
                        copy.wait_recv()
                for way in (0, 1):
                    if step > 1 and step - 1 <= steps_of(i, way):
                        ring[i, way, step - 1].wait_recv()
                    if step <= steps_of(i, way):
                        source = lines(part, place_of(way, step - 1))
                        ring[i, way, step] = send(
                            source, source, z_send.at[i, way, step - 1], z_recv.at[i, way, step - 1],
                            at_z((1, -1)[way]),
                        )
                for n, at in numbers(step, i):
                    if part == "b":
                        go_across(n, at)
                    else:
                        go_over(part, n, at)
        if 1 <= step - 3 <= zs // 2 + 1:
            for n, at in numbers(step - 3, 0):
                if n < 5:
                    arrange(n, at)

    slot(1)

    def poleward(store, which):
        return [
            send(store.at[pl.ds(HERE + OWN - RIM, RIM)], store.at[pl.ds(BAND, RIM)],
                 h_send.at[which, 0], h_recv.at[which, 0], near(0, 1)),
            send(store.at[pl.ds(HERE, RIM)], store.at[pl.ds(HERE + OWN, RIM)],
                 h_send.at[which, 1], h_recv.at[which, 1], near(0, -1)),
        ]

    def sideward(store, which):
        source = store.at[pl.ds(BAND, BAND)]
        return [
            send(source, store.at[pl.ds(0, BAND)], h_send.at[which, 2], h_recv.at[which, 2], near(1, 0)),
            send(source, store.at[pl.ds(2 * BAND, BAND)], h_send.at[which, 3], h_recv.at[which, 3], near(-1, 0)),
        ]

    halo = poleward(px, 0), poleward(cx, 1)
    cell = lax.broadcasted_iota(jnp.int32, (OWN, EXT), 0)
    other = lax.broadcasted_iota(jnp.int32, (OWN, EXT), 1)
    band = jnp.where(other >= BAND, 1, 0) + jnp.where(other >= 2 * BAND, 1, 0)
    rows = ((other - band * BAND) >> 3) - (cell >> 3)
    cols = (band - 1) * SIDE + (other & 7) - (cell & 7)
    inside = (rows >= 0) & (rows <= 2 * RAD) & (cols >= -RAD) & (cols <= RAD)
    other_row = ((other - band * BAND) >> 3) - RAD + first_row
    cell_row = (cell >> 3) + first_row
    bias[0] = jnp.where(inside & (other_row >= 0) & (other_row < lats), 0.0, -jnp.inf).astype(F32)
    bias[1] = jnp.where(
        inside & (cell_row < lats) & (other_row >= 0) & (other_row < SIDE * lats_dev), 0.0, -jnp.inf
    ).astype(F32)

    slot(2)
    slot(3)
    for copy in halo[0] + halo[1]:
        copy.wait_recv()
    halo = sideward(px, 0), sideward(cx, 1)
    for step in range(4, zs // 2 + 2):
        slot(step)

    def embed(n):
        rows_of = slice(n * BAND, (n + 1) * BAND)
        patch = dot_nt(px[rows_of], whole[0][...].reshape(width, pads))
        centred = patch - jnp.mean(patch, axis=-1, keepdims=True)
        inverse = lax.rsqrt(jnp.mean(centred * centred, axis=-1, keepdims=True) + EPS)
        normal = centred * inverse
        nx[rows_of] = normal.astype(BF16)
        if n == 1:
            emb[...] = patch[RIM : RIM + OWN]
            nor[...] = normal[RIM : RIM + OWN]
            inv[...] = jnp.broadcast_to(inverse[RIM : RIM + OWN], inv.shape)

    def project(weight, result):
        result[...] = dot_nt(nx[...], weight[...]).astype(BF16)

    for copy in halo[0]:
        copy.wait_recv()
    for n in range(zs):
        swap[0, n, 0].wait_recv()
    embed(0)
    slot(zs // 2 + 2)
    embed(1)
    embed(2)
    slot(zs // 2 + 3)
    for n, at in [(5, place_of(0, 3)), (6, place_of(1, 3)), (zs - 1, place_of(0, 4))]:
        arrange(n, at)
    for weight, result in ((wk, kx), (wq, qx), (wv, vx)):
        project(weight, result)
    at_o = half * SPLIT.index("o")

    def out_rows():
        return gb[:, :, :, :, at_o : at_o + half].reshape(width, half)

    for copy in halo[1]:
        copy.wait_recv()
    ext_row = lax.broadcasted_iota(jnp.int32, (BAND, 1), 0) // SIDE - RAD + first_row
    valid = jnp.where(ext_row < lats, 1.0, 0.0).astype(F32)
    gx[...] = (dot_nn(cx[...], out_rows()) * jnp.concatenate([valid] * 3, axis=0)).astype(BF16)

    scale = 1.0 / math.sqrt(wq.shape[0] // HEADS)
    pairs = HEADS // 2

    low = lax.broadcasted_iota(jnp.int32, (OWN, 128), 1) < 64
    none = jnp.zeros((OWN, 128), BF16)

    def apart(tile):
        return jnp.concatenate([jnp.where(low, tile, none), jnp.where(low, none, tile)], axis=0)

    def together(both):
        return jnp.where(low, both[:OWN], both[OWN:])

    lane = lax.broadcasted_iota(jnp.int32, (OWN, 128), 1)
    known = jnp.zeros((OWN, 128), F32)
    reach = jnp.concatenate([bias[0], bias[0]], axis=0)
    for p in range(pairs):
        tile = slice(p * 128, (p + 1) * 128)
        keys, values = kx[:, tile], vx[:, tile]
        scores = dot_nt(apart(qx[here, tile]), keys) * scale + reach
        top = jnp.max(scores, axis=-1, keepdims=True)
        terms = jnp.exp(scores - top)
        total = jnp.sum(terms, axis=-1, keepdims=True)
        prob = terms / total
        dprob = dot_nt(apart(gx[here, tile]), values)
        delta = jnp.sum(prob * dprob, axis=-1, keepdims=True)
        ds[p] = (prob * (dprob - delta)).astype(BF16)
        pb[p] = prob.astype(BF16)
        for place, column in ((0, top), (HEADS, total), (2 * HEADS, delta)):
            known = jnp.where(lane == place + 2 * p, column[:OWN], known)
            known = jnp.where(lane == place + 2 * p + 1, column[OWN:], known)

    turned = jnp.transpose(jnp.concatenate([known, jnp.zeros((OWN, 128), F32)], axis=0), (1, 0))
    sx[len(around)] = turned[: 3 * HEADS]
    told = [
        send(sx.at[len(around)], sx.at[n], f_send.at[n], f_recv.at[n], near(a, b)) for n, (a, b) in enumerate(around)
    ]
    reach = jnp.concatenate([bias[1], bias[1]], axis=0)
    for p in range(pairs):
        tile = slice(p * 128, (p + 1) * 128)
        att[:, tile] = together(dot_nn(pb[p], vx[:, tile])).astype(BF16)
        dq[:, tile] = together(dot_nn(ds[p], kx[:, tile]) * scale).astype(BF16)
        raw[p] = dot_nt(apart(kx[here, tile]), qx[:, tile]) * scale + reach
        rise[p] = dot_nt(apart(vx[here, tile]), gx[:, tile])
    slope_q = dot_nn(dq[...], wq[...])
    mixed = emb[...] + dot_nt(att[...], out_rows())
    own_row = lax.broadcasted_iota(jnp.int32, (OWN, 1), 0) // SIDE + first_row
    own_valid = jnp.where(own_row < lats, 1.0, 0.0).astype(F32)
    out_ref[...] = (mixed * own_valid).astype(BF16)
    for copy in told:
        copy.wait_recv()

    strips = []
    for a in (-1, 0, 1):
        for b in (-1, 0, 1):
            n = len(around) if (a, b) == (0, 0) else around.index((-a, -b))
            begin, end = {-1: (OWN - RIM, OWN), 0: (0, OWN), 1: (0, RIM)}[b]
            strips.append(sx[n][:, begin:end])
    facts = jnp.concatenate(strips, axis=1)
    for p in range(pairs):
        tile = slice(p * 128, (p + 1) * 128)

        def fact(place):
            first = jnp.broadcast_to(facts[place + 2 * p : place + 2 * p + 1, :EXT], (OWN, EXT))
            second = jnp.broadcast_to(facts[place + 2 * p + 1 : place + 2 * p + 2, :EXT], (OWN, EXT))
            return jnp.concatenate([first, second], axis=0)

        queries, grads = qx[:, tile], gx[:, tile]
        prob = jnp.exp(raw[p] - fact(0)) / fact(HEADS)
        dscore = (prob * (rise[p] - fact(2 * HEADS))).astype(BF16)
        dk[:, tile] = together(dot_nn(dscore, queries) * scale).astype(BF16)
        dv[:, tile] = together(dot_nn(prob.astype(BF16), grads)).astype(BF16)

    slope = slope_q + dot_nn(dk[...], wk[...]) + dot_nn(dv[...], wv[...])
    normal = nor[...]
    centre = jnp.mean(slope, axis=-1, keepdims=True)
    along = jnp.mean(slope * normal, axis=-1, keepdims=True)
    masked = cx[here].astype(F32) * own_valid
    grad_embed = (masked + inv[:, 0:1] * (slope - centre - normal * along)).astype(BF16)
    result = dot_nn(grad_embed, whole[0][...].reshape(width, pads)).astype(BF16)
    grad_ref[...] = result[:, 0:patch_width]

    for copy in sent:
        copy.wait_send()


def body(patches, query_weight, key_weight, value_weight, out_weight, embed_weight, cotangent):
    rows, cols, patch_width = patches.shape
    width = cotangent.shape[-1]
    lons, lats_dev = lax.axis_size("lon"), lax.axis_size("lat")
    zs = lons // 8
    channels = query_weight.shape[1] * lons
    wide_patch = -(-patch_width // 128) * 128
    blocks = (zs, 4, 2, 16)
    vmem = pltpu.VMEM
    dma = pltpu.SemaphoreType.DMA
    out, grad = pl.pallas_call(
        functools.partial(kernel, (lons, lats_dev)),
        out_shape=(
            jax.ShapeDtypeStruct((OWN, width), BF16),
            jax.ShapeDtypeStruct((OWN, patch_width), BF16),
        ),
        in_specs=[pl.BlockSpec(memory_space=pltpu.HBM)] * 7,
        out_specs=(pl.BlockSpec(memory_space=vmem),) * 2,
        scratch_shapes=[
            [vmem(blocks + (wide_patch if name == "e" else width // 2,), BF16) for name in WHOLE],
            vmem(blocks + (len(SPLIT) * (width // 2),), BF16),
            vmem((3, query_weight.shape[1], width), BF16),
            vmem((width // lons, channels), BF16),
            [vmem((OWN, patch_width), BF16), vmem((width // lons, patch_width), BF16)],
            vmem((len(SPLIT), width // lons, channels), BF16),
            vmem((channels, width), BF16),
            vmem((channels, width), BF16),
            vmem((channels, width), BF16),
            vmem((EXT, wide_patch), BF16),
            vmem((EXT, width), BF16),
            vmem((9, 3 * HEADS, 128), F32),
            vmem((EXT, width), BF16),
            vmem((EXT, channels), BF16),
            vmem((EXT, channels), BF16),
            vmem((EXT, channels), BF16),
            vmem((EXT, channels), BF16),
            vmem((OWN, width), F32),
            vmem((OWN, width), F32),
            vmem((OWN, 128), F32),
            vmem((OWN, channels), BF16),
            vmem((OWN, channels), BF16),
            vmem((OWN, channels), BF16),
            vmem((OWN, channels), BF16),
            vmem((2, OWN, EXT), F32),
            vmem((HEADS // 2, 2 * OWN, EXT), BF16),
            vmem((HEADS // 2, 2 * OWN, EXT), BF16),
            vmem((HEADS // 2, 2 * OWN, EXT), F32),
            vmem((HEADS // 2, 2 * OWN, EXT), F32),
            dma((len(WHOLE) + 1, 3)),
            dma((len(WHOLE) + 1, 3)),
            dma((len(WHOLE) + 1, 2, zs // 2)),
            dma((len(WHOLE) + 1, 2, zs // 2)),
            dma((zs, 3)),
            dma((zs, 3)),
            dma((len(WHOLE) + 1, zs, 4)),
            dma((len(WHOLE) + 1, zs, 4)),
            dma((2, 4)),
            dma((2, 4)),
            dma((8,)),
            dma((8,)),
            dma((7,)),
        ],
        compiler_params=pltpu.CompilerParams(
            collective_id=0, has_side_effects=True, vmem_limit_bytes=62 * 1024 * 1024
        ),
    )(
        patches.reshape(rows * cols, patch_width),
        query_weight.T,
        key_weight.T,
        value_weight.T,
        out_weight.T,
        embed_weight.T,
        cotangent.reshape(rows * cols, width),
    )
    return out.reshape(rows, cols, width), grad.reshape(rows, cols, patch_width)


def solution(mesh):
    in_specs = (
        P("lat", "lon", None),
        P(None, "lon"),
        P(None, "lon"),
        P(None, "lon"),
        P(None, "lon"),
        P(None, "lon"),
        P("lat", "lon", None),
    )
    out_specs = (P("lat", "lon", None), P("lat", "lon", None))
    return jax.shard_map(body, mesh=mesh, in_specs=in_specs, out_specs=out_specs, check_vma=False)
```
